512 devices in a mesh: dp: 128 (over x, z, core), narrow: 4 (over y).
Axes of the slice: x: 4, y: 4, z: 16, core: 2. Of those that a mesh axis runs over, the one named last changes fastest.
Arguments:
- grad_parts: bfloat16 [4, 192, 512, 512], P('narrow', None, 'dp')
- first_moment: float32 [192, 512, 512], P(None, 'dp', 'narrow'), may hold values from -320 to 320
- second_moment: float32 [192, 512, 512], P(None, 'dp', 'narrow'), may hold values from 0.25 to 4
- factors: float32 [128, 4, 512, 512], P('dp', 'narrow'), as said below
- block_order: int32 [192], replicated, may hold values from 0 to 191, each once
- owner_counts: int32 [128], replicated, may hold values from 0 to 2, as said below
Outputs:
- update: bfloat16 [192, 512, 512], P(None, 'dp', 'narrow')
- new_first: float32 [192, 512, 512], P(None, 'dp', 'narrow')
- new_second: float32 [192, 512, 512], P(None, 'dp', 'narrow')
- new_factors: float32 [128, 4, 512, 512], P('dp', 'narrow')
The draws below stay inside these ranges and needn't reach their ends.
Inputs may be any that keep to these rules, and one draw needn't show every extreme that they name: owner_counts sum to 192; owner o's blocks are block_order[start[o]] to block_order[start[o] + owner_counts[o] - 1], with start[o] the sum of the counts of lower owners; some owner holds none and some holds 2. `factors`: every block of a statistic is symmetric, with a positive diagonal larger than the sum of magnitudes of the rest of its row.
All inputs are finite; a program needn't handle non-finite values.
Results may differ from the reference program's by a relative error of at most 0.0023.
The reference program's roundings to bfloat16 on the way count: a program that leaves them out, or rounds other values in their place, can miss the bound.
Values may be sent and summed in bfloat16 or wider, within the bound.
No kernel may reach another device: no remote copies, remote signals or barrier semaphores. Data moves between devices by JAX's collectives and lax.ppermute only.
A program may use at most 128 MiB of HBM per device.

```python
import math
import jax
import jax.numpy as jnp
from jax import lax

B = 512
ITERS = 2
SLOTS = 2
NBLK = 192
N_DP = 128
N_NARROW = 4


def ranked_scales(key, count, length):
    keys = jax.random.split(key, count)
    ranks = jax.vmap(lambda single: jax.random.permutation(single, length))(keys)
    return 8.0 / jnp.sqrt(ranks.astype(jnp.float32) + 1.0)


def draw_grad_parts(key, part):
    key = jax.random.fold_in(key, 31)
    key_rows = jax.random.fold_in(key, 0)
    key_cols = jax.random.fold_in(key, 1)
    key_own = jax.random.fold_in(key, 3)
    row_scale = ranked_scales(key_rows, NBLK, B)
    col_scale = ranked_scales(key_cols, NBLK, B)
    noise = jnp.clip(jax.random.normal(key_own, (N_NARROW, NBLK, B, B), jnp.float32), -4.0, 4.0)
    return (noise * row_scale[None, :, :, None] * col_scale[None, :, None, :]).astype(jnp.bfloat16)


def strip_weights(key, heavy_lo, heavy_hi):
    key_pick, key_heavy = jax.random.split(key)
    strip = (jnp.arange(B, dtype=jnp.int32) // (B // N_DP)).astype(jnp.int32)
    chosen = jax.random.randint(key_pick, (NBLK,), 0, N_DP)
    heavy = jax.random.uniform(key_heavy, (NBLK, 1), jnp.float32, heavy_lo, heavy_hi)
    rising = 1.0 + 2.0 * strip.astype(jnp.float32) / (N_DP - 1)
    boost = jnp.where(strip[None, :] == chosen[:, None], heavy, 1.0)
    return boost * rising[None, :]


def draw_first_moment(key, part):
    key = jax.random.fold_in(key, 41)
    key_noise, key_strip = jax.random.split(key)
    noise = jnp.clip(jax.random.normal(key_noise, (NBLK, B, B), jnp.float32), -4.0, 4.0)
    weights = strip_weights(key_strip, 14.0, 26.0)
    return noise * weights[:, :, None]


def draw_factors(key, part):
    key = jax.random.fold_in(key, 11)
    key_noise, key_level = jax.random.split(key)
    spread = 0.2
    level_lo = 0.45
    level_hi = 0.8
    noise = jax.random.uniform(key_noise, (N_DP, N_NARROW, B, B), jnp.float32, -1.0, 1.0)
    symmetric = (noise + jnp.swapaxes(noise, 2, 3)) * spread
    level = jnp.exp(jax.random.uniform(key_level, (N_DP, N_NARROW, B), jnp.float32, jnp.log(level_lo), jnp.log(level_hi))) * B
    identity = jnp.eye(B, dtype=jnp.float32)
    return symmetric * (1.0 - identity) + identity * level[:, :, :, None]


def draw_owner_counts(key, part):
    key = jax.random.fold_in(key, 23)
    spots = jnp.arange(N_DP, dtype=jnp.int32)
    base = jnp.where(spots < N_DP // 8, 0, jnp.where(spots < 3 * N_DP // 8, 1, 2)).astype(jnp.int32)
    return jax.random.permutation(key, base)


def steps_of(own_key, shape, shards, smallest, top_value):
    gain = 1.0
    for dim, parts in shards:
        draws = jax.random.uniform(jax.random.fold_in(jax.random.fold_in(own_key, 6), dim), (parts,), jnp.float32, smallest / len(shards), top_value / len(shards))
        gain = gain * jnp.repeat(jnp.exp(draws), shape[dim] // parts).reshape((-1,) + (1,) * (len(shape) - 1 - dim))
    return gain


def setup_inputs(seed: int = 0) -> dict:
    key_list = jax.random.split(jax.random.key(seed), 7)
    return {
        "grad_parts": draw_grad_parts(jax.random.fold_in(key_list[6], 71), 0),
        "first_moment": draw_first_moment(jax.random.fold_in(key_list[6], 71), 0),
        "second_moment": jnp.clip(jnp.exp(math.log(4.0) - 2.7725887 * jax.random.uniform(key_list[2], (NBLK, B, B), jnp.float32) ** steps_of(key_list[2], (NBLK, B, B), ((1, 128), (2, 4)), -0.2, 0.2)), 0.25, 4.0),
        "factors": draw_factors(jax.random.fold_in(key_list[6], 71), 0),
        "block_order": jax.random.permutation(key_list[4], NBLK).astype(jnp.int32),
        "owner_counts": draw_owner_counts(jax.random.fold_in(key_list[6], 71), 0),
    }


def inverse_root(statistic):
    frob_norm = jnp.sqrt(jnp.sum(statistic * statistic))
    identity = jnp.eye(statistic.shape[0], dtype=statistic.dtype)
    current = statistic / frob_norm
    root_iter = identity
    for sweep in range(ITERS):
        step_term = (5.0 * identity - current) * 0.25
        root_iter = jnp.dot(root_iter, step_term, precision=lax.Precision.HIGHEST, preferred_element_type=jnp.float32)
        squared = jnp.dot(step_term, step_term, precision=lax.Precision.HIGHEST, preferred_element_type=jnp.float32)
        fourth = jnp.dot(squared, squared, precision=lax.Precision.HIGHEST, preferred_element_type=jnp.float32)
        current = jnp.dot(fourth, current, precision=lax.Precision.HIGHEST, preferred_element_type=jnp.float32)
    return root_iter * frob_norm ** (-0.25)

def slot_tables(block_order, owner_counts, slot_total):
    block_total = block_order.shape[0]
    end_points = jnp.cumsum(owner_counts).astype(jnp.int32)
    start_points = end_points - owner_counts
    slot_range = jnp.arange(slot_total, dtype=jnp.int32)
    filled = slot_range[None, :] < owner_counts[:, None]
    list_index = jnp.minimum(start_points[:, None] + slot_range[None, :], block_total - 1)
    blocks = block_order[list_index]
    position = jnp.zeros((block_total,), jnp.int32).at[block_order].set(jnp.arange(block_total, dtype=jnp.int32))
    owner_of = lax.optimization_barrier(jnp.sum((end_points[None, :] <= position[:, None]).astype(jnp.int32), axis=1))
    slot_of = position - start_points[owner_of]
    return (blocks, filled, owner_of, slot_of)

def reference(grad_parts, first_moment, second_moment, factors, block_order, owner_counts):
    gradient = lax.optimization_barrier(jnp.sum(grad_parts.astype(jnp.float32), axis=0))
    new_first = 0.9 * first_moment + 0.1 * gradient
    new_second = 0.95 * second_moment + 0.05 * gradient * gradient
    adam_dir = new_first / (jnp.sqrt(new_second) + 1e-08)
    adam_sq = lax.optimization_barrier(jnp.sum(adam_dir * adam_dir, axis=(1, 2)))
    grad_half = gradient.astype(jnp.bfloat16)
    blocks, filled, owner_of, slot_of = slot_tables(block_order, owner_counts, SLOTS)

    def per_owner(packed):
        slot_blocks, slot_filled, previous = packed
        matrices = jnp.where(slot_filled[:, None, None], grad_half[slot_blocks], jnp.zeros((), jnp.bfloat16))
        statistics = []
        root_list = []
        for member in range(N_NARROW):
            matrix = matrices[member // 2]
            turned = matrix if member % 2 == 0 else matrix.T
            product = jnp.dot(turned, turned.T, preferred_element_type=jnp.float32)
            statistic = 0.9 * previous[member] + 0.1 * product
            statistics.append(statistic)
            root_list.append(inverse_root(statistic).astype(jnp.bfloat16))
        updates = []
        for slot_number in range(SLOTS):
            inner_term = jnp.dot(matrices[slot_number], root_list[2 * slot_number + 1], preferred_element_type=jnp.float32).astype(jnp.bfloat16)
            precond = jnp.dot(root_list[2 * slot_number], inner_term, preferred_element_type=jnp.float32)
            prec_norm = jnp.sqrt(jnp.sum(precond * precond))
            adam_norm = jnp.sqrt(jnp.where(slot_filled[slot_number], adam_sq[slot_blocks[slot_number]], 0.0))
            updates.append((precond * (adam_norm / (prec_norm + 1e-06))).astype(jnp.bfloat16))
        return (jnp.stack(statistics), jnp.stack(updates))
    new_factors, all_updates = lax.map(per_owner, (blocks, filled, factors))
    update = all_updates[owner_of, slot_of]
    return (update, new_first, new_second, new_factors)
```

```python
import jax
import jax.numpy as jnp
from jax import lax
from jax.experimental import pallas as pl
from jax.experimental.pallas import tpu as pltpu
from jax.sharding import PartitionSpec as P

BLOCKS = 192
OWNERS = 128
NARROW = 4
ROWS = 4
COLS = 128
ORDER = 512
GROUP = 10
BF16 = jnp.bfloat16
F32 = jnp.float32
VMEM = pl.BlockSpec(memory_space=pltpu.VMEM)
SMEM = pl.BlockSpec(memory_space=pltpu.SMEM)
POLY = (1.5625, -1101.25 / 1024.0, 781.25 / 1024.0, -312.5 / 1024.0, 62.5 / 1024.0, -6.25 / 1024.0, 0.25 / 1024.0)


def three_terms(value):
    high = value.astype(BF16).astype(F32)
    rest = value - high
    middle = rest.astype(BF16).astype(F32)
    return high, middle, (rest - middle).astype(BF16).astype(F32)


def moments_kernel(order, counts, parts, first, second, new_first, new_second, out, grads, sums, slots):
    gradient = jnp.sum(parts[...].astype(F32), axis=0)
    moment = 0.9 * first[...] + 0.1 * gradient
    new_first[...] = moment
    variance = 0.95 * second[...] + 0.05 * gradient * gradient
    new_second[...] = variance
    adam = moment / (jnp.sqrt(variance) + 1e-08)
    pairs = BLOCKS // 2
    gradient = gradient.reshape(pairs, 8, COLS)
    grads[:pairs] = gradient
    grads[pairs:, 0:4] = gradient[:, 4:8]
    grads[pairs:, 4:8] = gradient[:, 0:4]
    squares = (adam * adam).reshape(pairs, 8, COLS)
    lane = lax.broadcasted_iota(jnp.int32, (pairs, 1, COLS), 2)
    for half in range(2):
        total = jnp.sum(squares[:, 4 * half : 4 * half + 4], axis=1, keepdims=True)
        total = jnp.sum(total, axis=2, keepdims=True)
        high, middle, low = three_terms(jnp.broadcast_to(total, (pairs, 1, COLS)))
        third = jnp.where(lane >= 3, lane - 3, lane)
        sums[half] = jnp.where(third == 0, high, jnp.where(third == 1, middle, low))

    row = lax.broadcasted_iota(jnp.int32, (8, COLS), 0)
    across = lax.broadcasted_iota(jnp.int32, (1, COLS), 1)

    def four_owners(step, start):
        base = pl.multiple_of(step * (4 * GROUP), 8)
        for k in range(4):
            count = counts[step * 4 + k]
            block0 = order[jnp.minimum(start, BLOCKS - 1)]
            block1 = order[jnp.minimum(start + 1, BLOCKS - 1)]
            half0, half1 = block0 & 1, block1 & 1
            rows0 = grads[(block0 >> 1) + pairs * half0]
            rows1 = grads[(block1 >> 1) + pairs * (1 - half1)]
            both = jnp.where(row < ROWS, rows0, rows1)
            slots[pl.ds(base + GROUP * k, 8)] = jnp.where(row < ROWS * count, both, 0.0)
            totals = jnp.where(across < 3, sums[half0, block0 >> 1], sums[half1, block1 >> 1])
            totals = jnp.where(across < 3 * count, totals, 0.0)
            slots[pl.ds(base + GROUP * k + 8, 2)] = jnp.broadcast_to(totals, (2, COLS))
            start = start + count
        return start

    lax.fori_loop(0, OWNERS // 4, four_owners, jnp.int32(0))
    out[...] = slots[...].astype(BF16)


def spread_kernel(arrived, out, wide, halves):
    wide[...] = arrived[...].astype(F32)

    def four_sources(step, total):
        base = pl.multiple_of(step * (4 * GROUP), 8)
        for k in range(4):
            at = base + GROUP * k
            halves[0, pl.ds(step * 16 + ROWS * k, ROWS)] = wide[pl.ds(at, ROWS)]
            halves[1, pl.ds(step * 16 + ROWS * k, ROWS)] = wide[pl.ds(at + ROWS, ROWS)]
            total = total + wide[pl.ds(at + 8, 1)]
        return total

    total = lax.fori_loop(0, OWNERS // 4, four_sources, jnp.zeros((1, COLS), F32))
    across = lax.broadcasted_iota(jnp.int32, (1, COLS), 1)
    for slot in range(2):
        block = halves[slot].astype(BF16)
        mine = (across >= 3 * slot) & (across < 3 * slot + 3)
        sum_sq = jnp.sum(jnp.where(mine, total, 0.0), axis=1, keepdims=True)
        high, middle, low = three_terms(jnp.broadcast_to(sum_sq, (1, COLS)))
        pieces = jnp.where(across == 0, high, jnp.where(across == 1, middle, jnp.where(across == 2, low, 0.0)))
        pieces = jnp.broadcast_to(pieces, (16, COLS)).astype(BF16)
        for member in (2 * slot, 2 * slot + 1):
            out[member, 0:ORDER] = block
            out[member, ORDER : ORDER + 16] = pieces


def product(left, right, contract):
    return lax.dot_general(left, right, (contract, ((), ())), preferred_element_type=F32)


def two_terms(value):
    high = value.astype(BF16)
    return high, (value - high.astype(F32)).astype(BF16)


def float_product(left, right):
    high0, low0 = left
    high1, low1 = right
    plain = ((1,), (0,))
    return product(high0, high1, plain) + (product(high0, low1, plain) + product(low0, high1, plain))


def root_of(statistic):
    norm = jnp.sqrt(jnp.sum(jnp.sum(statistic * statistic, axis=0, keepdims=True), axis=1, keepdims=True))
    matrix = statistic / norm
    matrix_terms = two_terms(matrix)
    square = float_product(matrix_terms, matrix_terms)
    cube = float_product(matrix_terms, two_terms(square))
    above = POLY[4] * matrix + POLY[5] * square + POLY[6] * cube
    top = float_product(two_terms(cube), two_terms(above))
    row = lax.broadcasted_iota(jnp.int32, (ORDER, ORDER), 0)
    col = lax.broadcasted_iota(jnp.int32, (ORDER, ORDER), 1)
    value = POLY[1] * matrix + POLY[2] * square + (POLY[3] * cube + top)
    value = value + jnp.where(row == col, POLY[0], 0.0)
    return (value * lax.rsqrt(jnp.sqrt(norm))).astype(BF16)


def owner_kernel(member_ref, chunks, mine, other, new_mine, kept, passed, grad, turned, left, right, result):
    member = member_ref[0]
    is_right = (member & 1) == 1
    for n in range(NARROW):
        grad[:, COLS * n : COLS * (n + 1)] = chunks[n, 0:ORDER]
    adam_sq = jnp.zeros((1, COLS), F32)
    for n in range(NARROW):
        adam_sq = adam_sq + chunks[n, ORDER : ORDER + 16].astype(F32)[0:1]
    adam_sq = jnp.sum(adam_sq, axis=1, keepdims=True)

    def sides(left_factor, right_factor):
        block = grad[...]
        left_stat = 0.9 * left_factor[...] + 0.1 * product(block, block, ((1,), (1,)))
        left[...] = root_of(left_stat)
        right_stat = 0.9 * right_factor[...] + 0.1 * product(block, block, ((0,), (0,)))
        right[...] = root_of(right_stat)
        return left_stat, right_stat

    @pl.when(jnp.logical_not(is_right))
    def _():
        new_mine[...] = sides(mine, other)[0]

    @pl.when(is_right)
    def _():
        new_mine[...] = sides(other, mine)[1]

    inner = product(grad[...], right[...], ((1,), (0,))).astype(BF16)
    precond = product(left[...], inner, ((1,), (0,)))
    square = jnp.sum(jnp.sum(precond * precond, axis=0, keepdims=True), axis=1, keepdims=True)
    scale = jnp.sqrt(adam_sq) / (jnp.sqrt(square) + 1e-06)
    result[...] = precond * scale
    kept[...] = result[:, pl.ds(pl.multiple_of(member * COLS, COLS), COLS)].astype(BF16)
    passed[...] = result[:, pl.ds(pl.multiple_of((NARROW - 1 - member) * COLS, COLS), COLS)].astype(BF16)


def place_kernel(order, counts, member_ref, arrived, update, wide, blocks):
    wide[...] = arrived[...].astype(F32).reshape(2, OWNERS // 2, 8, COLS)
    flip = member_ref[0] >> 1

    def two_owners(step, start):
        for k in range(2):
            count = counts[step * 2 + k]
            for slot in range(2):
                rows = wide[slot ^ flip, step, ROWS * k : ROWS * (k + 1)]
                filled = count > slot
                block = order[jnp.minimum(start + slot, BLOCKS - 1)]
                blocks[jnp.where(filled, block, BLOCKS), 0:ROWS] = rows
            start = start + count
        return start

    lax.fori_loop(0, OWNERS // 2, two_owners, jnp.int32(0))
    packed = blocks[0:BLOCKS].reshape(BLOCKS // 2, 2, 8, COLS)
    joined = jnp.concatenate([packed[:, 0, 0:ROWS], packed[:, 1, 0:ROWS]], axis=1)
    update[...] = joined.reshape(BLOCKS * ROWS, COLS).astype(BF16)


def call(kernel, in_specs, out_shapes, scratch, vmem_mib, flops, moved):
    return pl.pallas_call(
        kernel,
        in_specs=in_specs,
        out_specs=[VMEM] * len(out_shapes),
        out_shape=out_shapes,
        scratch_shapes=scratch,
        compiler_params=pltpu.CompilerParams(vmem_limit_bytes=vmem_mib * 1024 * 1024),
        cost_estimate=pl.CostEstimate(flops=flops, bytes_accessed=moved, transcendentals=0),
    )


def per_device(grad_parts, first_moment, second_moment, factors, block_order, owner_counts):
    member = lax.axis_index("narrow").astype(jnp.int32).reshape(1)
    shape = jax.ShapeDtypeStruct
    flat = BLOCKS * ROWS

    partial_cols = grad_parts[0].reshape(BLOCKS, ROWS, NARROW, COLS).transpose(2, 0, 1, 3)
    partial_cols = lax.all_to_all(partial_cols, "narrow", 0, 0, tiled=True)

    factor, partial_cols = lax.optimization_barrier((factors[0, 0], partial_cols))
    other_factor = lax.ppermute(factor, "narrow", [(0, 1), (1, 0), (2, 3), (3, 2)])

    new_first, new_second, outgoing = call(
        moments_kernel,
        [SMEM, SMEM, VMEM, VMEM, VMEM],
        [shape((flat, COLS), F32), shape((flat, COLS), F32), shape((OWNERS * GROUP, COLS), BF16)],
        [
            pltpu.VMEM((BLOCKS, 8, COLS), F32),
            pltpu.VMEM((2, BLOCKS // 2, 1, COLS), F32),
            pltpu.VMEM((OWNERS * GROUP, COLS), F32),
        ],
        16,
        4_000_000,
        2_800_000,
    )(
        block_order,
        owner_counts,
        partial_cols.reshape(NARROW, flat, COLS),
        first_moment.reshape(flat, COLS),
        second_moment.reshape(flat, COLS),
    )

    arrived = lax.all_to_all(outgoing.reshape(OWNERS, GROUP // 2, 2, COLS), "dp", 0, 0, tiled=True)
    (spread,) = call(
        spread_kernel,
        [VMEM],
        [shape((NARROW, ORDER + 16, COLS), BF16)],
        [pltpu.VMEM((OWNERS * GROUP, COLS), F32), pltpu.VMEM((2, ORDER, COLS), F32)],
        16,
        1_000_000,
        900_000,
    )(arrived.reshape(OWNERS * GROUP, COLS))
    chunks = lax.all_to_all(spread, "narrow", 0, 0, tiled=True)

    new_factor, kept, passed = call(
        owner_kernel,
        [SMEM, VMEM, VMEM, VMEM],
        [shape((ORDER, ORDER), F32), shape((ORDER, COLS), BF16), shape((ORDER, COLS), BF16)],
        [pltpu.VMEM((ORDER, ORDER), BF16)] * 4 + [pltpu.VMEM((ORDER, ORDER), F32)],
        40,
        6_000_000_000,
        4_000_000,
    )(member, chunks, factor, other_factor)

    received = lax.ppermute(passed, "narrow", [(0, 3), (3, 0), (1, 2), (2, 1)])
    outgoing = jnp.stack([kept, received]).reshape(2, OWNERS, ROWS, COLS)
    came_back = lax.all_to_all(outgoing, "dp", 1, 1, tiled=True)
    (update,) = call(
        place_kernel,
        [SMEM, SMEM, SMEM, VMEM],
        [shape((flat, COLS), BF16)],
        [pltpu.VMEM((2, OWNERS // 2, 8, COLS), F32), pltpu.VMEM((BLOCKS + 8, 8, COLS), F32)],
        16,
        1_000_000,
        500_000,
    )(block_order, owner_counts, member, came_back.reshape(2, ORDER, COLS))
    local = (BLOCKS, ROWS, COLS)
    return update.reshape(local), new_first.reshape(local), new_second.reshape(local), new_factor[None, None]


def solution(mesh):
    return jax.shard_map(
        per_device,
        mesh=mesh,
        in_specs=(
            P("narrow", None, "dp", None),
            P(None, "dp", "narrow"),
            P(None, "dp", "narrow"),
            P("dp", "narrow", None, None),
            P(),
            P(),
        ),
        out_specs=(
            P(None, "dp", "narrow"),
            P(None, "dp", "narrow"),
            P(None, "dp", "narrow"),
            P("dp", "narrow", None, None),
        ),
        check_vma=False,
    )
```

```python
import jax
import jax.numpy as jnp
from jax import lax
from jax.experimental import pallas as pl
from jax.experimental.pallas import tpu as pltpu
from jax.sharding import PartitionSpec as P

BLOCKS = 192
OWNERS = 128
NARROW = 4
ROWS = 4
COLS = 128
ORDER = 512
GROUP = 10
BF16 = jnp.bfloat16
F32 = jnp.float32
VMEM = pl.BlockSpec(memory_space=pltpu.VMEM)
SMEM = pl.BlockSpec(memory_space=pltpu.SMEM)
ANY = pl.BlockSpec(memory_space=pl.ANY)
PAIRS = BLOCKS // 2
EMPTY = BLOCKS
POLY = (1.5625, -1101.25 / 1024.0, 781.25 / 1024.0, -312.5 / 1024.0, 62.5 / 1024.0, -6.25 / 1024.0, 0.25 / 1024.0)


def three_terms(value):
    high = value.astype(BF16).astype(F32)
    rest = value - high
    middle = rest.astype(BF16).astype(F32)
    return high, middle, (rest - middle).astype(BF16).astype(F32)


def columns_kernel(parts, out, sem):
    copies = [
        pltpu.make_async_copy(parts.at[:, :, pl.ds(COLS * n, COLS)], out.at[n], sem.at[n]) for n in range(NARROW)
    ]
    for copy in copies:
        copy.start()
    for copy in copies:
        copy.wait()


def table_kernel(order, counts, table):
    def step(index, start):
        for k in range(8):
            owner = index * 8 + k
            count = counts[owner]
            for slot in range(2):
                block = order[jnp.minimum(start + slot, BLOCKS - 1)]
                filled = count > slot
                half = (block & 1) if slot == 0 else 1 - (block & 1)
                table[slot * OWNERS + owner] = jnp.where(filled, (block >> 1) + PAIRS * half, EMPTY)
                table[(2 + slot) * OWNERS + owner] = jnp.where(filled, block, EMPTY)
            start = start + count
        return start

    lax.fori_loop(0, OWNERS // 8, step, jnp.int32(0))


def moments_kernel(
    table, parts, first, second, new_first, new_second, out, entries, slots, moment_held, variance_held, sem
):
    gradient = jnp.sum(parts[...].astype(F32), axis=0)
    moment = 0.9 * first[...] + 0.1 * gradient
    variance = 0.95 * second[...] + 0.05 * gradient * gradient
    moment_held[...] = moment
    variance_held[...] = variance
    copies = [
        pltpu.make_async_copy(moment_held, new_first, sem.at[0]),
        pltpu.make_async_copy(variance_held, new_second, sem.at[1]),
    ]
    for copy in copies:
        copy.start()
    adam = moment / (jnp.sqrt(variance) + 1e-08)
    gradient = gradient.reshape(PAIRS, 8, COLS)
    entries[:PAIRS, 0:8] = gradient
    entries[PAIRS : 2 * PAIRS, 0:4] = gradient[:, 4:8]
    entries[PAIRS : 2 * PAIRS, 4:8] = gradient[:, 0:4]
    squares = (adam * adam).reshape(PAIRS, 8, COLS)
    upper = lax.broadcasted_iota(jnp.int32, (1, 8, COLS), 1) < ROWS
    fore = lax.broadcasted_iota(jnp.int32, (1, 8, COLS), 2) < 3
    row_sums = jnp.sum(squares, axis=2, keepdims=True)
    lane = lax.broadcasted_iota(jnp.int32, (1, 1, COLS), 2)
    term = jnp.where(lane >= 3, lane - 3, lane)
    for half in range(2):
        pick = (upper == fore) if half == 0 else (upper != fore)
        total = jnp.sum(jnp.where(pick, row_sums, 0.0), axis=1, keepdims=True)
        high, middle, low = three_terms(total)
        pieces = jnp.where(term == 0, high, jnp.where(term == 1, middle, low))
        entries[PAIRS * half : PAIRS * (half + 1), 8:9] = pieces
    entries[EMPTY] = jnp.zeros((16, COLS), F32)
    row = lax.broadcasted_iota(jnp.int32, (8, COLS), 0)
    across = lax.broadcasted_iota(jnp.int32, (1, COLS), 1)

    def four_owners(step, carry):
        base = pl.multiple_of(step * (4 * GROUP), 8)
        for k in range(4):
            entry0 = table[step * 4 + k]
            entry1 = table[OWNERS + step * 4 + k]
            slots[pl.ds(base + GROUP * k, 8)] = jnp.where(row < ROWS, entries[entry0, 0:8], entries[entry1, 0:8])
            totals = jnp.where(across < 3, entries[entry0, 8:9], entries[entry1, 8:9])
            slots[pl.ds(base + GROUP * k + 8, 2)] = jnp.broadcast_to(totals, (2, COLS))
        return carry

    lax.fori_loop(0, OWNERS // 4, four_owners, 0)
    out[...] = slots[...].astype(BF16)
    for copy in copies:
        copy.wait()


def spread_kernel(arrived, out):
    groups = arrived[...].astype(F32).reshape(OWNERS // 4, 4 * GROUP, COLS)
    starts = [GROUP * k for k in range(4)]
    total = jnp.sum(sum(groups[:, at + 8 : at + 9] for at in starts), axis=0)
    across = lax.broadcasted_iota(jnp.int32, (1, COLS), 1)
    for slot in range(2):
        rows = [groups[:, at + ROWS * slot : at + ROWS * (slot + 1)] for at in starts]
        block = jnp.concatenate(rows, axis=1).reshape(ORDER, COLS).astype(BF16)
        mine = (across >= 3 * slot) & (across < 3 * slot + 3)
        sum_sq = jnp.sum(jnp.where(mine, total, 0.0), axis=1, keepdims=True)
        high, middle, low = three_terms(jnp.broadcast_to(sum_sq, (1, COLS)))
        pieces = jnp.where(across == 0, high, jnp.where(across == 1, middle, jnp.where(across == 2, low, 0.0)))
        pieces = jnp.broadcast_to(pieces, (16, COLS)).astype(BF16)
        for member in (2 * slot, 2 * slot + 1):
            out[member, 0:ORDER] = block
            out[member, ORDER : ORDER + 16] = pieces


def product(left, right, contract=((1,), (0,))):
    return lax.dot_general(left, right, (contract, ((), ())), preferred_element_type=F32)


def two_terms(value):
    high = value.astype(BF16)
    return high, (value - high.astype(F32)).astype(BF16)


def sum_of_squares(parts):
    total = sum(jnp.sum((part * part).reshape(-1, 8, ORDER), axis=0) for part in parts)
    return jnp.sum(jnp.sum(total, axis=0, keepdims=True), axis=1, keepdims=True)


def owner_kernel(
    member_ref, chunks, mine, other, new_mine, kept, passed, grad, stats, lefts, rights, later, squares, outer, cubes, roots, inner, result
):
    member = member_ref[0]
    is_right = (member & 1) == 1
    halves = [slice(0, ORDER // 2), slice(ORDER // 2, ORDER)]
    for n in range(NARROW):
        grad[:, COLS * n : COLS * (n + 1)] = chunks[n, 0:ORDER]
    adam_sq = sum(chunks[n, ORDER : ORDER + 16].astype(F32)[0:1] for n in range(NARROW))
    adam_sq = jnp.sum(adam_sq, axis=1, keepdims=True)

    def statistics(left_factor, right_factor, side):
        for rows in halves:
            left = 0.9 * left_factor[rows].astype(F32) + 0.1 * product(grad[rows], grad[...], ((1,), (1,)))
            stats[0, rows] = left
            if side == 0:
                new_mine[rows] = left
        for rows in halves:
            right = 0.9 * right_factor[rows].astype(F32) + 0.1 * product(grad[:, rows], grad[...], ((0,), (0,)))
            stats[1, rows] = right
            if side == 1:
                new_mine[rows] = right

    @pl.when(jnp.logical_not(is_right))
    def _():
        statistics(mine, other, 0)

    @pl.when(is_right)
    def _():
        statistics(other, mine, 1)

    norms = [jnp.sqrt(sum_of_squares([stats[side, rows] for rows in halves])) for side in range(2)]
    inverses = [1.0 / norm for norm in norms]

    def put_right(target, side, rows, high, low):
        for third, term in enumerate((high, low, high)):
            target[side, third * ORDER + rows.start : third * ORDER + rows.stop] = term

    for side in range(2):
        for rows in halves:
            high, low = two_terms(stats[side, rows] * inverses[side])
            for third, term in enumerate((high, high, low)):
                lefts[side, rows, third * ORDER : (third + 1) * ORDER] = term
            put_right(rights, side, rows, high, low)
    for side in range(2):
        for rows in halves:
            square = product(lefts[side, rows], rights[side])
            squares[side, rows] = square
            put_right(later, side, rows, *two_terms(square))
    for side in range(2):
        for rows in halves:
            cube = product(lefts[side, rows], later[side])
            matrix = stats[side, rows] * inverses[side]
            square = squares[side, rows]
            outer[side, rows] = (POLY[4] * matrix + POLY[5] * square + POLY[6] * cube).astype(BF16)
            cubes[side, rows] = cube.astype(BF16)
            row = lax.broadcasted_iota(jnp.int32, (ORDER // 2, ORDER), 0) + rows.start
            col = lax.broadcasted_iota(jnp.int32, (ORDER // 2, ORDER), 1)
            value = POLY[1] * matrix + POLY[2] * square + POLY[3] * cube
            squares[side, rows] = value + jnp.where(row == col, POLY[0], 0.0)
    for side in range(2):
        scale = lax.rsqrt(jnp.sqrt(norms[side]))
        for rows in halves:
            value = squares[side, rows] + product(cubes[side, rows], outer[side])
            roots[side, rows] = (value * scale).astype(BF16)
    for rows in halves:
        inner[rows] = product(grad[rows], roots[1]).astype(BF16)
    for rows in halves:
        result[rows] = product(roots[0, rows], inner[...])
    square = sum_of_squares([result[rows] for rows in halves])
    scale = jnp.sqrt(adam_sq) / (jnp.sqrt(square) + 1e-06)
    kept[...] = (result[:, pl.ds(pl.multiple_of(member * COLS, COLS), COLS)] * scale).astype(BF16)
    passed[...] = (result[:, pl.ds(pl.multiple_of((NARROW - 1 - member) * COLS, COLS), COLS)] * scale).astype(BF16)


def place_kernel(table, member_ref, arrived, update, wide, blocks):
    wide[...] = arrived[...].astype(F32).reshape(2, OWNERS // 2, 8, COLS)
    flip = member_ref[0] >> 1

    def eight_owners(step, carry):
        for k in range(8):
            for slot in range(2):
                block = table[(2 + slot) * OWNERS + step * 8 + k]
                first_row = ROWS * (k % 2)
                blocks[block] = wide[slot ^ flip, step * 4 + k // 2, first_row : first_row + ROWS]
        return carry

    lax.fori_loop(0, OWNERS // 8, eight_owners, 0)
    update[...] = blocks[0:BLOCKS].reshape(BLOCKS * ROWS, COLS).astype(BF16)


def call(kernel, in_specs, outs, scratch, vmem_mib, flops, moved):
    specs, shapes = zip(*outs)
    return pl.pallas_call(
        kernel,
        in_specs=in_specs,
        out_specs=list(specs),
        out_shape=[jax.ShapeDtypeStruct(*shape) for shape in shapes],
        scratch_shapes=scratch,
        compiler_params=pltpu.CompilerParams(vmem_limit_bytes=vmem_mib * 1024 * 1024),
        cost_estimate=pl.CostEstimate(flops=flops, bytes_accessed=moved, transcendentals=0),
    )


def per_device(grad_parts, first_moment, second_moment, factors, block_order, owner_counts):
    member = lax.axis_index("narrow").astype(jnp.int32).reshape(1)
    flat = BLOCKS * ROWS

    (partial_cols,) = call(
        columns_kernel,
        [ANY],
        [(VMEM, ((NARROW, BLOCKS, ROWS, COLS), BF16))],
        [pltpu.SemaphoreType.DMA((NARROW,))],
        16,
        0,
        1_600_000,
    )(grad_parts[0])
    partial_cols, block_order, owner_counts = lax.optimization_barrier((partial_cols, block_order, owner_counts))
    (table,) = call(table_kernel, [SMEM, SMEM], [(SMEM, ((4 * OWNERS,), jnp.int32))], [], 16, 0, 8_000_000)(
        block_order, owner_counts
    )
    partial_cols = lax.all_to_all(partial_cols, "narrow", 0, 0, tiled=True)

    factor, partial_cols = lax.optimization_barrier((factors[0, 0], partial_cols))
    other_factor = lax.ppermute(factor.astype(BF16), "narrow", [(0, 1), (1, 0), (2, 3), (3, 2)])

    new_first, new_second, outgoing = call(
        moments_kernel,
        [SMEM, VMEM, VMEM, VMEM],
        [(ANY, ((flat, COLS), F32)), (ANY, ((flat, COLS), F32)), (VMEM, ((OWNERS * GROUP, COLS), BF16))],
        [
            pltpu.VMEM((BLOCKS + 1, 16, COLS), F32),
            pltpu.VMEM((OWNERS * GROUP, COLS), F32),
            pltpu.VMEM((flat, COLS), F32),
            pltpu.VMEM((flat, COLS), F32),
            pltpu.SemaphoreType.DMA((2,)),
        ],
        16,
        4_000_000,
        2_800_000,
    )(
        table,
        partial_cols.reshape(NARROW, flat, COLS),
        first_moment.reshape(flat, COLS),
        second_moment.reshape(flat, COLS),
    )

    arrived = lax.all_to_all(outgoing.reshape(OWNERS, GROUP // 2, 2, COLS), "dp", 0, 0, tiled=True)
    (spread,) = call(
        spread_kernel,
        [VMEM],
        [(VMEM, ((NARROW, ORDER + 16, COLS), BF16))],
        [],
        16,
        1_000_000,
        900_000,
    )(arrived.reshape(OWNERS * GROUP, COLS))
    chunks = lax.all_to_all(spread, "narrow", 0, 0, tiled=True)

    square = (ORDER, ORDER)
    new_factor, kept, passed = call(
        owner_kernel,
        [SMEM, VMEM, VMEM, VMEM],
        [(VMEM, (square, F32)), (VMEM, ((ORDER, COLS), BF16)), (VMEM, ((ORDER, COLS), BF16))],
        [
            pltpu.VMEM(square, BF16),
            pltpu.VMEM((2, *square), F32),
            pltpu.VMEM((2, ORDER, 3 * ORDER), BF16),
            pltpu.VMEM((2, 3 * ORDER, ORDER), BF16),
            pltpu.VMEM((2, 3 * ORDER, ORDER), BF16),
            pltpu.VMEM((2, *square), F32),
            pltpu.VMEM((2, *square), BF16),
            pltpu.VMEM((2, *square), BF16),
            pltpu.VMEM((2, *square), BF16),
            pltpu.VMEM(square, BF16),
            pltpu.VMEM(square, F32),
        ],
        27,
        5_000_000_000,
        4_000_000,
    )(member, chunks, factor, other_factor)

    received = lax.ppermute(passed, "narrow", [(0, 3), (3, 0), (1, 2), (2, 1)])
    outgoing = jnp.stack([kept, received]).reshape(2, OWNERS, ROWS, COLS)
    came_back = lax.all_to_all(outgoing, "dp", 1, 1, tiled=True)
    (update,) = call(
        place_kernel,
        [SMEM, SMEM, VMEM],
        [(VMEM, ((flat, COLS), BF16))],
        [pltpu.VMEM((2, OWNERS // 2, 8, COLS), F32), pltpu.VMEM((BLOCKS + 8, ROWS, COLS), F32)],
        16,
        1_000_000,
        500_000,
    )(table, member, came_back.reshape(2, ORDER, COLS))
    local = (BLOCKS, ROWS, COLS)
    return update.reshape(local), new_first.reshape(local), new_second.reshape(local), new_factor[None, None]


def solution(mesh):
    return jax.shard_map(
        per_device,
        mesh=mesh,
        in_specs=(
            P("narrow", None, "dp", None),
            P(None, "dp", "narrow"),
            P(None, "dp", "narrow"),
            P("dp", "narrow", None, None),
            P(),
            P(),
        ),
        out_specs=(
            P(None, "dp", "narrow"),
            P(None, "dp", "narrow"),
            P(None, "dp", "narrow"),
            P("dp", "narrow", None, None),
        ),
        check_vma=False,
    )
```

```python
import jax
import jax.numpy as jnp
from jax import lax
from jax.experimental import pallas as pl
from jax.experimental.pallas import tpu as pltpu
from jax.sharding import Mesh, PartitionSpec as P

BLOCKS = 192
OWNERS = 128
NARROW = 4
ROWS = 4
COLS = 128
ORDER = 512
CORES = 2
CHIPS = OWNERS // CORES
GROUP = 18
HALF = CHIPS * ROWS
BF16 = jnp.bfloat16
F32 = jnp.float32
VMEM = pl.BlockSpec(memory_space=pltpu.VMEM)
SMEM = pl.BlockSpec(memory_space=pltpu.SMEM)
ANY = pl.BlockSpec(memory_space=pl.ANY)
PAIRS = BLOCKS // 2
EMPTY = BLOCKS
POLY = (1.5625, -1101.25 / 1024.0, 781.25 / 1024.0, -312.5 / 1024.0, 62.5 / 1024.0, -6.25 / 1024.0, 0.25 / 1024.0)


def three_terms(value):
    high = value.astype(BF16).astype(F32)
    rest = value - high
    middle = rest.astype(BF16).astype(F32)
    return high, middle, (rest - middle).astype(BF16).astype(F32)


def columns_kernel(parts, out, sem):
    copies = [
        pltpu.make_async_copy(parts.at[:, :, pl.ds(COLS * n, COLS)], out.at[n], sem.at[n]) for n in range(NARROW)
    ]
    for copy in copies:
        copy.start()
    for copy in copies:
        copy.wait()


def table_kernel(order, counts, table):
    def step(index, start):
        for k in range(8):
            owner = index * 8 + k
            count = counts[owner]
            for slot in range(2):
                block = order[jnp.minimum(start + slot, BLOCKS - 1)]
                filled = count > slot
                half = (block & 1) if slot == 0 else 1 - (block & 1)
                table[slot * OWNERS + owner] = jnp.where(filled, (block >> 1) + PAIRS * half, EMPTY)
                table[(2 + slot) * OWNERS + owner] = jnp.where(filled, block, EMPTY)
            start = start + count
        return start

    lax.fori_loop(0, OWNERS // 8, step, jnp.int32(0))


def moments_kernel(
    table, parts, first, second, new_first, new_second, out, entries, slots, moment_held, variance_held, sem
):
    gradient = jnp.sum(parts[...].astype(F32), axis=0)
    moment = 0.9 * first[...] + 0.1 * gradient
    variance = 0.95 * second[...] + 0.05 * gradient * gradient
    moment_held[...] = moment
    variance_held[...] = variance
    copies = [
        pltpu.make_async_copy(moment_held, new_first, sem.at[0]),
        pltpu.make_async_copy(variance_held, new_second, sem.at[1]),
    ]
    for copy in copies:
        copy.start()
    adam = moment / (jnp.sqrt(variance) + 1e-08)
    gradient = gradient.reshape(PAIRS, 8, COLS)
    entries[:PAIRS, 0:8] = gradient
    entries[PAIRS : 2 * PAIRS, 0:4] = gradient[:, 4:8]
    entries[PAIRS : 2 * PAIRS, 4:8] = gradient[:, 0:4]
    squares = (adam * adam).reshape(PAIRS, 8, COLS)
    upper = lax.broadcasted_iota(jnp.int32, (1, 8, COLS), 1) < ROWS
    wide_lane = lax.broadcasted_iota(jnp.int32, (1, 8, COLS), 2)
    fore = (wide_lane < 3) | ((wide_lane >= 6) & (wide_lane < 9))
    row_sums = jnp.sum(squares, axis=2, keepdims=True)
    lane = lax.broadcasted_iota(jnp.int32, (1, 1, COLS), 2)
    term = sum(jnp.where(lane >= at, -3, 0) for at in (3, 6, 9)) + lane
    for half in range(2):
        pick = (upper == fore) if half == 0 else (upper != fore)
        total = jnp.sum(jnp.where(pick, row_sums, 0.0), axis=1, keepdims=True)
        high, middle, low = three_terms(total)
        pieces = jnp.where(term == 0, high, jnp.where(term == 1, middle, low))
        entries[PAIRS * half : PAIRS * (half + 1), 8:9] = pieces
    entries[EMPTY] = jnp.zeros((16, COLS), F32)
    row = lax.broadcasted_iota(jnp.int32, (8, COLS), 0)
    across = lax.broadcasted_iota(jnp.int32, (1, COLS), 1)

    def four_chips(step, carry):
        base = pl.multiple_of(step * (4 * GROUP), 8)
        for k in range(4):
            at = base + GROUP * k
            totals = []
            for core in range(CORES):
                owner = (step * 4 + k) * CORES + core
                entry0, entry1 = table[owner], table[OWNERS + owner]
                slots[pl.ds(at + 8 * core, 8)] = jnp.where(row < ROWS, entries[entry0, 0:8], entries[entry1, 0:8])
                totals += [entries[entry0, 8:9], entries[entry1, 8:9]]
            first_owner = jnp.where(across < 3, totals[0], totals[1])
            second_owner = jnp.where(across < 9, totals[2], totals[3])
            totals = jnp.where(across < 6, first_owner, second_owner)
            slots[pl.ds(at + 16, 2)] = jnp.broadcast_to(totals, (2, COLS))
        return carry

    lax.fori_loop(0, CHIPS // 4, four_chips, 0)
    out[...] = slots[...].astype(BF16)
    for copy in copies:
        copy.wait()


def spread_kernel(arrived, out):
    groups = arrived[...].astype(F32).reshape(CHIPS // 4, 4 * GROUP, COLS)
    starts = [GROUP * k for k in range(4)]
    total = jnp.sum(sum(groups[:, at + 16 : at + 17] for at in starts), axis=0)
    across = lax.broadcasted_iota(jnp.int32, (1, COLS), 1)
    for core in range(CORES):
        for slot in range(2):
            place = 2 * core + slot
            rows = [groups[:, at + ROWS * place : at + ROWS * (place + 1)] for at in starts]
            block = jnp.concatenate(rows, axis=1).reshape(HALF, COLS).astype(BF16)
            mine = (across >= 3 * place) & (across < 3 * place + 3)
            sum_sq = jnp.sum(jnp.where(mine, total, 0.0), axis=1, keepdims=True)
            high, middle, low = three_terms(jnp.broadcast_to(sum_sq, (1, COLS)))
            pieces = jnp.where(across == 0, high, jnp.where(across == 1, middle, jnp.where(across == 2, low, 0.0)))
            pieces = jnp.broadcast_to(pieces, (16, COLS)).astype(BF16)
            for member in (2 * slot, 2 * slot + 1):
                out[NARROW * core + member, 0:HALF] = block
                out[NARROW * core + member, HALF : HALF + 16] = pieces


def product(left, right, contract=((1,), (0,))):
    return lax.dot_general(left, right, (contract, ((), ())), preferred_element_type=F32)


def two_terms(value):
    high = value.astype(BF16)
    return high, (value - high.astype(F32)).astype(BF16)


def sum_of_squares(parts):
    total = sum(jnp.sum((part * part).reshape(-1, 8, ORDER), axis=0) for part in parts)
    return jnp.sum(jnp.sum(total, axis=0, keepdims=True), axis=1, keepdims=True)


def owner_kernel(
    member_ref, chunks, mine, other, new_mine, kept, passed, grad, stats, lefts, rights, later, squares, outer, cubes, roots, inner, result
):
    member = member_ref[0]
    is_right = (member & 1) == 1
    halves = [slice(0, ORDER // 2), slice(ORDER // 2, ORDER)]
    for n in range(NARROW):
        rows = [chunks[NARROW * core + n, 0:HALF].astype(F32).reshape(CHIPS, ROWS, COLS) for core in range(CORES)]
        grad[:, COLS * n : COLS * (n + 1)] = jnp.concatenate(rows, axis=1).reshape(ORDER, COLS).astype(BF16)
    adam_sq = sum(chunks[k, HALF : HALF + 16].astype(F32)[0:1] for k in range(CORES * NARROW))
    adam_sq = jnp.sum(adam_sq, axis=1, keepdims=True)

    def statistics(left_factor, right_factor, side):
        for rows in halves:
            left = 0.9 * left_factor[rows].astype(F32) + 0.1 * product(grad[rows], grad[...], ((1,), (1,)))
            stats[0, rows] = left
            if side == 0:
                new_mine[rows] = left
        for rows in halves:
            right = 0.9 * right_factor[rows].astype(F32) + 0.1 * product(grad[:, rows], grad[...], ((0,), (0,)))
            stats[1, rows] = right
            if side == 1:
                new_mine[rows] = right

    @pl.when(jnp.logical_not(is_right))
    def _():
        statistics(mine, other, 0)

    @pl.when(is_right)
    def _():
        statistics(other, mine, 1)

    norms = [jnp.sqrt(sum_of_squares([stats[side, rows] for rows in halves])) for side in range(2)]
    inverses = [1.0 / norm for norm in norms]

    def put_right(target, side, rows, high, low):
        for third, term in enumerate((high, low, high)):
            target[side, third * ORDER + rows.start : third * ORDER + rows.stop] = term

    for side in range(2):
        for rows in halves:
            high, low = two_terms(stats[side, rows] * inverses[side])
            for third, term in enumerate((high, high, low)):
                lefts[side, rows, third * ORDER : (third + 1) * ORDER] = term
            put_right(rights, side, rows, high, low)
    for side in range(2):
        for rows in halves:
            square = product(lefts[side, rows], rights[side])
            squares[side, rows] = square
            put_right(later, side, rows, *two_terms(square))
    for side in range(2):
        for rows in halves:
            cube = product(lefts[side, rows], later[side])
            matrix = stats[side, rows] * inverses[side]
            square = squares[side, rows]
            outer[side, rows] = (POLY[4] * matrix + POLY[5] * square + POLY[6] * cube).astype(BF16)
            cubes[side, rows] = cube.astype(BF16)
            row = lax.broadcasted_iota(jnp.int32, (ORDER // 2, ORDER), 0) + rows.start
            col = lax.broadcasted_iota(jnp.int32, (ORDER // 2, ORDER), 1)
            value = POLY[1] * matrix + POLY[2] * square + POLY[3] * cube
            squares[side, rows] = value + jnp.where(row == col, POLY[0], 0.0)
    for side in range(2):
        scale = lax.rsqrt(jnp.sqrt(norms[side]))
        for rows in halves:
            value = squares[side, rows] + product(cubes[side, rows], outer[side])
            roots[side, rows] = (value * scale).astype(BF16)
    for rows in halves:
        inner[rows] = product(grad[rows], roots[1]).astype(BF16)
    for rows in halves:
        result[rows] = product(roots[0, rows], inner[...])
    square = sum_of_squares([result[rows] for rows in halves])
    scale = jnp.sqrt(adam_sq) / (jnp.sqrt(square) + 1e-06)
    kept[...] = (result[:, pl.ds(pl.multiple_of(member * COLS, COLS), COLS)] * scale).astype(BF16)
    passed[...] = (result[:, pl.ds(pl.multiple_of((NARROW - 1 - member) * COLS, COLS), COLS)] * scale).astype(BF16)


def place_kernel(table, member_ref, arrived, update, wide, blocks):
    wide[...] = arrived[...].astype(F32).reshape(2, OWNERS // 2, 8, COLS)
    flip = member_ref[0] >> 1

    def eight_owners(step, carry):
        for k in range(8):
            for slot in range(2):
                block = table[(2 + slot) * OWNERS + step * 8 + k]
                first_row = ROWS * (k % 2)
                blocks[block] = wide[slot ^ flip, step * 4 + k // 2, first_row : first_row + ROWS]
        return carry

    lax.fori_loop(0, OWNERS // 8, eight_owners, 0)
    update[...] = blocks[0:BLOCKS].reshape(BLOCKS * ROWS, COLS).astype(BF16)


def call(kernel, in_specs, outs, scratch, vmem_mib, flops, moved):
    specs, shapes = zip(*outs)
    return pl.pallas_call(
        kernel,
        in_specs=in_specs,
        out_specs=list(specs),
        out_shape=[jax.ShapeDtypeStruct(*shape) for shape in shapes],
        scratch_shapes=scratch,
        compiler_params=pltpu.CompilerParams(vmem_limit_bytes=vmem_mib * 1024 * 1024),
        cost_estimate=pl.CostEstimate(flops=flops, bytes_accessed=moved, transcendentals=0),
    )


def per_device(grad_parts, first_moment, second_moment, factors, block_order, owner_counts):
    member = lax.axis_index("narrow").astype(jnp.int32).reshape(1)
    flat = BLOCKS * ROWS

    (partial_cols,) = call(
        columns_kernel,
        [ANY],
        [(VMEM, ((NARROW, BLOCKS, ROWS, COLS), BF16))],
        [pltpu.SemaphoreType.DMA((NARROW,))],
        16,
        0,
        1_600_000,
    )(grad_parts[0])
    partial_cols, block_order, owner_counts = lax.optimization_barrier((partial_cols, block_order, owner_counts))
    (table,) = call(table_kernel, [SMEM, SMEM], [(SMEM, ((4 * OWNERS,), jnp.int32))], [], 16, 0, 8_000_000)(
        block_order, owner_counts
    )
    partial_cols = lax.all_to_all(partial_cols, "narrow", 0, 0, tiled=True)

    factor, partial_cols = lax.optimization_barrier((factors[0, 0], partial_cols))
    other_factor = lax.ppermute(factor.astype(BF16), "narrow", [(0, 1), (1, 0), (2, 3), (3, 2)])

    new_first, new_second, outgoing = call(
        moments_kernel,
        [SMEM, VMEM, VMEM, VMEM],
        [(ANY, ((flat, COLS), F32)), (ANY, ((flat, COLS), F32)), (VMEM, ((CHIPS * GROUP, COLS), BF16))],
        [
            pltpu.VMEM((BLOCKS + 1, 16, COLS), F32),
            pltpu.VMEM((CHIPS * GROUP, COLS), F32),
            pltpu.VMEM((flat, COLS), F32),
            pltpu.VMEM((flat, COLS), F32),
            pltpu.SemaphoreType.DMA((2,)),
        ],
        16,
        4_000_000,
        2_800_000,
    )(
        table,
        partial_cols.reshape(NARROW, flat, COLS),
        first_moment.reshape(flat, COLS),
        second_moment.reshape(flat, COLS),
    )

    arrived = lax.all_to_all(outgoing.reshape(CHIPS, GROUP // 2, 2, COLS), "chip", 0, 0, tiled=True)
    (spread,) = call(
        spread_kernel,
        [VMEM],
        [(VMEM, ((CORES * NARROW, HALF + 16, COLS), BF16))],
        [],
        16,
        1_000_000,
        900_000,
    )(arrived.reshape(CHIPS * GROUP, COLS))
    chunks = lax.all_to_all(spread, ("core", "narrow"), 0, 0, tiled=True)

    square = (ORDER, ORDER)
    new_factor, kept, passed = call(
        owner_kernel,
        [SMEM, VMEM, VMEM, VMEM],
        [(VMEM, (square, F32)), (VMEM, ((ORDER, COLS), BF16)), (VMEM, ((ORDER, COLS), BF16))],
        [
            pltpu.VMEM(square, BF16),
            pltpu.VMEM((2, *square), F32),
            pltpu.VMEM((2, ORDER, 3 * ORDER), BF16),
            pltpu.VMEM((2, 3 * ORDER, ORDER), BF16),
            pltpu.VMEM((2, 3 * ORDER, ORDER), BF16),
            pltpu.VMEM((2, *square), F32),
            pltpu.VMEM((2, *square), BF16),
            pltpu.VMEM((2, *square), BF16),
            pltpu.VMEM((2, *square), BF16),
            pltpu.VMEM(square, BF16),
            pltpu.VMEM(square, F32),
        ],
        27,
        5_000_000_000,
        4_000_000,
    )(member, chunks, factor, other_factor)

    received = lax.ppermute(passed, "narrow", [(0, 3), (3, 0), (1, 2), (2, 1)])
    outgoing = jnp.stack([kept, received]).reshape(2, OWNERS, ROWS, COLS)
    came_back = lax.all_to_all(outgoing, ("chip", "core"), 1, 1, tiled=True)
    (update,) = call(
        place_kernel,
        [SMEM, SMEM, VMEM],
        [(VMEM, ((flat, COLS), BF16))],
        [pltpu.VMEM((2, OWNERS // 2, 8, COLS), F32), pltpu.VMEM((BLOCKS + 8, ROWS, COLS), F32)],
        16,
        1_000_000,
        500_000,
    )(table, member, came_back.reshape(2, ORDER, COLS))
    local = (BLOCKS, ROWS, COLS)
    return update.reshape(local), new_first.reshape(local), new_second.reshape(local), new_factor[None, None]


def solution(mesh):
    devices = mesh.devices.reshape(CHIPS, CORES, NARROW)
    rows = ("chip", "core")
    moments = P(None, rows, "narrow")
    factors = P(rows, "narrow", None, None)
    return jax.shard_map(
        per_device,
        mesh=Mesh(devices, ("chip", "core", "narrow")),
        in_specs=(P("narrow", None, rows, None), moments, moments, factors, P(), P()),
        out_specs=(moments, moments, moments, factors),
        check_vma=False,
    )
```

```python
import jax
import jax.numpy as jnp
from jax import lax
from jax.experimental import pallas as pl
from jax.experimental.pallas import tpu as pltpu
from jax.sharding import Mesh, PartitionSpec as P

BLOCKS = 192
OWNERS = 128
NARROW = 4
ROWS = 4
COLS = 128
ORDER = 512
CORES = 2
CHIPS = OWNERS // CORES
GROUP = 18
HALF = CHIPS * ROWS
BF16 = jnp.bfloat16
F32 = jnp.float32
VMEM = pl.BlockSpec(memory_space=pltpu.VMEM)
SMEM = pl.BlockSpec(memory_space=pltpu.SMEM)
ANY = pl.BlockSpec(memory_space=pl.ANY)
PAIRS = BLOCKS // 2
EMPTY = BLOCKS
POLY = (1.5625, -1101.25 / 1024.0, 781.25 / 1024.0, -312.5 / 1024.0, 62.5 / 1024.0, -6.25 / 1024.0, 0.25 / 1024.0)


def three_terms(value):
    high = value.astype(BF16).astype(F32)
    rest = value - high
    middle = rest.astype(BF16).astype(F32)
    return high, middle, (rest - middle).astype(BF16).astype(F32)


def columns_kernel(parts, out, sem):
    copies = [
        pltpu.make_async_copy(parts.at[:, :, pl.ds(COLS * n, COLS)], out.at[n], sem.at[n]) for n in range(NARROW)
    ]
    for copy in copies:
        copy.start()
    for copy in copies:
        copy.wait()


def table_kernel(order, counts, table):
    def step(index, start):
        for k in range(8):
            owner = index * 8 + k
            count = counts[owner]
            for slot in range(2):
                block = order[jnp.minimum(start + slot, BLOCKS - 1)]
                filled = count > slot
                half = (block & 1) if slot == 0 else 1 - (block & 1)
                table[slot * OWNERS + owner] = jnp.where(filled, (block >> 1) + PAIRS * half, EMPTY)
                table[(2 + slot) * OWNERS + owner] = jnp.where(filled, block, EMPTY)
            start = start + count
        return start

    lax.fori_loop(0, OWNERS // 8, step, jnp.int32(0))


def moments_kernel(
    table, parts, first, second, new_first, new_second, out, entries, slots, moment_held, variance_held, sem
):
    gradient = jnp.sum(parts[...].astype(F32), axis=0)
    moment = 0.9 * first[...] + 0.1 * gradient
    variance = 0.95 * second[...] + 0.05 * gradient * gradient
    moment_held[...] = moment
    variance_held[...] = variance
    copies = [
        pltpu.make_async_copy(moment_held, new_first, sem.at[0]),
        pltpu.make_async_copy(variance_held, new_second, sem.at[1]),
    ]
    for copy in copies:
        copy.start()
    adam = moment / (jnp.sqrt(variance) + 1e-08)
    gradient = gradient.reshape(PAIRS, 8, COLS)
    entries[:PAIRS, 0:8] = gradient
    entries[PAIRS : 2 * PAIRS, 0:4] = gradient[:, 4:8]
    entries[PAIRS : 2 * PAIRS, 4:8] = gradient[:, 0:4]
    squares = (adam * adam).reshape(PAIRS, 8, COLS)
    upper = lax.broadcasted_iota(jnp.int32, (1, 8, COLS), 1) < ROWS
    wide_lane = lax.broadcasted_iota(jnp.int32, (1, 8, COLS), 2)
    fore = (wide_lane < 3) | ((wide_lane >= 6) & (wide_lane < 9))
    row_sums = jnp.sum(squares, axis=2, keepdims=True)
    lane = lax.broadcasted_iota(jnp.int32, (1, 1, COLS), 2)
    term = sum(jnp.where(lane >= at, -3, 0) for at in (3, 6, 9)) + lane
    for half in range(2):
        pick = (upper == fore) if half == 0 else (upper != fore)
        total = jnp.sum(jnp.where(pick, row_sums, 0.0), axis=1, keepdims=True)
        high, middle, low = three_terms(total)
        pieces = jnp.where(term == 0, high, jnp.where(term == 1, middle, low))
        entries[PAIRS * half : PAIRS * (half + 1), 8:9] = pieces
    entries[EMPTY] = jnp.zeros((16, COLS), F32)
    row = lax.broadcasted_iota(jnp.int32, (8, COLS), 0)
    across = lax.broadcasted_iota(jnp.int32, (1, COLS), 1)

    def four_chips(step, carry):
        base = pl.multiple_of(step * (4 * GROUP), 8)
        for k in range(4):
            at = base + GROUP * k
            totals = []
            for core in range(CORES):
                owner = (step * 4 + k) * CORES + core
                entry0, entry1 = table[owner], table[OWNERS + owner]
                slots[pl.ds(at + 8 * core, 8)] = jnp.where(row < ROWS, entries[entry0, 0:8], entries[entry1, 0:8])
                totals += [entries[entry0, 8:9], entries[entry1, 8:9]]
            first_owner = jnp.where(across < 3, totals[0], totals[1])
            second_owner = jnp.where(across < 9, totals[2], totals[3])
            totals = jnp.where(across < 6, first_owner, second_owner)
            slots[pl.ds(at + 16, 2)] = jnp.broadcast_to(totals, (2, COLS))
        return carry

    lax.fori_loop(0, CHIPS // 4, four_chips, 0)
    out[...] = slots[...].astype(BF16)
    for copy in copies:
        copy.wait()


def spread_kernel(arrived, out):
    groups = arrived[...].astype(F32).reshape(CHIPS // 4, 4 * GROUP, COLS)
    starts = [GROUP * k for k in range(4)]
    total = jnp.sum(sum(groups[:, at + 16 : at + 17] for at in starts), axis=0)
    across = lax.broadcasted_iota(jnp.int32, (1, COLS), 1)
    for core in range(CORES):
        for slot in range(2):
            place = 2 * core + slot
            rows = [groups[:, at + ROWS * place : at + ROWS * (place + 1)] for at in starts]
            block = jnp.concatenate(rows, axis=1).reshape(HALF, COLS).astype(BF16)
            mine = (across >= 3 * place) & (across < 3 * place + 3)
            sum_sq = jnp.sum(jnp.where(mine, total, 0.0), axis=1, keepdims=True)
            high, middle, low = three_terms(jnp.broadcast_to(sum_sq, (1, COLS)))
            pieces = jnp.where(across == 0, high, jnp.where(across == 1, middle, jnp.where(across == 2, low, 0.0)))
            pieces = jnp.broadcast_to(pieces, (16, COLS)).astype(BF16)
            for member in (2 * slot, 2 * slot + 1):
                out[NARROW * core + member, 0:HALF] = block
                out[NARROW * core + member, HALF : HALF + 16] = pieces


def product(left, right, contract=((1,), (0,))):
    return lax.dot_general(left, right, (contract, ((), ())), preferred_element_type=F32)


def two_terms(value):
    high = value.astype(BF16)
    return high, (value - high.astype(F32)).astype(BF16)


def sum_of_squares(parts):
    total = sum(jnp.sum((part * part).reshape(-1, 8, ORDER), axis=0) for part in parts)
    return jnp.sum(jnp.sum(total, axis=0, keepdims=True), axis=1, keepdims=True)


def owner_kernel(
    place_ref, chunks, mine, other, new_mine, outgoing, grad, stats, lefts, rights, later, squares, outer, cubes, roots, inner, result
):
    here, core = place_ref[0], place_ref[1]
    is_right = here == 1
    halves = [slice(0, ORDER // 2), slice(ORDER // 2, ORDER)]
    for n in range(NARROW):
        rows = [chunks[NARROW * core + n, 0:HALF].astype(F32).reshape(CHIPS, ROWS, COLS) for core in range(CORES)]
        grad[:, COLS * n : COLS * (n + 1)] = jnp.concatenate(rows, axis=1).reshape(ORDER, COLS).astype(BF16)
    adam_sq = sum(chunks[k, HALF : HALF + 16].astype(F32)[0:1] for k in range(CORES * NARROW))
    adam_sq = jnp.sum(adam_sq, axis=1, keepdims=True)

    def statistics(left_factor, right_factor, side):
        for rows in halves:
            left = 0.9 * left_factor[rows].astype(F32) + 0.1 * product(grad[rows], grad[...], ((1,), (1,)))
            stats[0, rows] = left
            if side == 0:
                new_mine[rows] = left
        for rows in halves:
            right = 0.9 * right_factor[rows].astype(F32) + 0.1 * product(grad[:, rows], grad[...], ((0,), (0,)))
            stats[1, rows] = right
            if side == 1:
                new_mine[rows] = right

    @pl.when(jnp.logical_not(is_right))
    def _():
        statistics(mine, other, 0)

    @pl.when(is_right)
    def _():
        statistics(other, mine, 1)

    norms = [jnp.sqrt(sum_of_squares([stats[side, rows] for rows in halves])) for side in range(2)]
    inverses = [1.0 / norm for norm in norms]

    def put_right(target, side, rows, high, low):
        for third, term in enumerate((high, low, high)):
            target[side, third * ORDER + rows.start : third * ORDER + rows.stop] = term

    for side in range(2):
        for rows in halves:
            high, low = two_terms(stats[side, rows] * inverses[side])
            for third, term in enumerate((high, high, low)):
                lefts[side, rows, third * ORDER : (third + 1) * ORDER] = term
            put_right(rights, side, rows, high, low)
    for side in range(2):
        for rows in halves:
            square = product(lefts[side, rows], rights[side])
            squares[side, rows] = square
            put_right(later, side, rows, *two_terms(square))
    for side in range(2):
        for rows in halves:
            cube = product(lefts[side, rows], later[side])
            matrix = stats[side, rows] * inverses[side]
            square = squares[side, rows]
            outer[side, rows] = (POLY[4] * matrix + POLY[5] * square + POLY[6] * cube).astype(BF16)
            cubes[side, rows] = cube.astype(BF16)
            row = lax.broadcasted_iota(jnp.int32, (ORDER // 2, ORDER), 0) + rows.start
            col = lax.broadcasted_iota(jnp.int32, (ORDER // 2, ORDER), 1)
            value = POLY[1] * matrix + POLY[2] * square + POLY[3] * cube
            squares[side, rows] = value + jnp.where(row == col, POLY[0], 0.0)
    for side in range(2):
        scale = lax.rsqrt(jnp.sqrt(norms[side]))
        for rows in halves:
            value = squares[side, rows] + product(cubes[side, rows], outer[side])
            roots[side, rows] = (value * scale).astype(BF16)
    for rows in halves:
        inner[rows] = product(grad[rows], roots[1]).astype(BF16)
    for rows in halves:
        result[rows] = product(roots[0, rows], inner[...])
    square = sum_of_squares([result[rows] for rows in halves])
    scale = jnp.sqrt(adam_sq) / (jnp.sqrt(square) + 1e-06)
    for pair in range(2):
        cols = result[:, pl.ds(pl.multiple_of((2 * pair + here) * COLS, COLS), COLS)] * scale
        cols = cols.reshape(CHIPS, CORES * ROWS, COLS)
        lower, upper = cols[:, 0:ROWS], cols[:, ROWS : 2 * ROWS]
        staying = jnp.where(core == 0, lower, upper).reshape(HALF, COLS)
        crossing = jnp.where(core == 0, upper, lower).reshape(HALF, COLS)
        outgoing[0, pair * HALF : (pair + 1) * HALF] = staying.astype(BF16)
        outgoing[1, pair * HALF : (pair + 1) * HALF] = crossing.astype(BF16)


def place_kernel(table, place_ref, stayed, crossed, update, wide, blocks):
    wide[0] = stayed[...].astype(F32).reshape(OWNERS // 2, 8, COLS)
    wide[1] = crossed[...].astype(F32).reshape(OWNERS // 2, 8, COLS)
    here = place_ref[1]

    def four_chips(step, carry):
        for k in range(4):
            for core in range(CORES):
                for slot in range(2):
                    block = table[(2 + slot) * OWNERS + (step * 4 + k) * CORES + core]
                    group = slot * (CHIPS // 2) + step * 2 + k // 2
                    first_row = ROWS * (k % 2)
                    blocks[block] = wide[core ^ here, group, first_row : first_row + ROWS]
        return carry

    lax.fori_loop(0, CHIPS // 4, four_chips, 0)
    update[...] = blocks[0:BLOCKS].reshape(BLOCKS * ROWS, COLS).astype(BF16)


def call(kernel, in_specs, outs, scratch, vmem_mib, flops, moved):
    specs, shapes = zip(*outs)
    return pl.pallas_call(
        kernel,
        in_specs=in_specs,
        out_specs=list(specs),
        out_shape=[jax.ShapeDtypeStruct(*shape) for shape in shapes],
        scratch_shapes=scratch,
        compiler_params=pltpu.CompilerParams(vmem_limit_bytes=vmem_mib * 1024 * 1024),
        cost_estimate=pl.CostEstimate(flops=flops, bytes_accessed=moved, transcendentals=0),
    )


def per_device(grad_parts, first_moment, second_moment, factors, block_order, owner_counts):
    place = jnp.stack([lax.axis_index("side"), lax.axis_index("core")]).astype(jnp.int32)
    flat = BLOCKS * ROWS

    (partial_cols,) = call(
        columns_kernel,
        [ANY],
        [(VMEM, ((NARROW, BLOCKS, ROWS, COLS), BF16))],
        [pltpu.SemaphoreType.DMA((NARROW,))],
        16,
        0,
        1_600_000,
    )(grad_parts[0])
    partial_cols, block_order, owner_counts = lax.optimization_barrier((partial_cols, block_order, owner_counts))
    (table,) = call(table_kernel, [SMEM, SMEM], [(SMEM, ((4 * OWNERS,), jnp.int32))], [], 16, 0, 8_000_000)(
        block_order, owner_counts
    )
    partial_cols = lax.all_to_all(partial_cols, ("pair", "side"), 0, 0, tiled=True)

    factor, partial_cols = lax.optimization_barrier((factors[0, 0], partial_cols))
    other_factor = lax.ppermute(factor.astype(BF16), "side", [(0, 1), (1, 0)])

    new_first, new_second, outgoing = call(
        moments_kernel,
        [SMEM, VMEM, VMEM, VMEM],
        [(ANY, ((flat, COLS), F32)), (ANY, ((flat, COLS), F32)), (VMEM, ((CHIPS * GROUP, COLS), BF16))],
        [
            pltpu.VMEM((BLOCKS + 1, 16, COLS), F32),
            pltpu.VMEM((CHIPS * GROUP, COLS), F32),
            pltpu.VMEM((flat, COLS), F32),
            pltpu.VMEM((flat, COLS), F32),
            pltpu.SemaphoreType.DMA((2,)),
        ],
        16,
        4_000_000,
        2_800_000,
    )(
        table,
        partial_cols.reshape(NARROW, flat, COLS),
        first_moment.reshape(flat, COLS),
        second_moment.reshape(flat, COLS),
    )

    arrived = lax.all_to_all(outgoing.reshape(CHIPS, GROUP // 2, 2, COLS), "chip", 0, 0, tiled=True)
    (spread,) = call(
        spread_kernel,
        [VMEM],
        [(VMEM, ((CORES * NARROW, HALF + 16, COLS), BF16))],
        [],
        16,
        1_000_000,
        900_000,
    )(arrived.reshape(CHIPS * GROUP, COLS))
    chunks = lax.all_to_all(spread, ("core", "pair", "side"), 0, 0, tiled=True)

    square = (ORDER, ORDER)
    new_factor, outgoing = call(
        owner_kernel,
        [SMEM, VMEM, VMEM, VMEM],
        [(VMEM, (square, F32)), (VMEM, ((2, ORDER, COLS), BF16))],
        [
            pltpu.VMEM(square, BF16),
            pltpu.VMEM((2, *square), F32),
            pltpu.VMEM((2, ORDER, 3 * ORDER), BF16),
            pltpu.VMEM((2, 3 * ORDER, ORDER), BF16),
            pltpu.VMEM((2, 3 * ORDER, ORDER), BF16),
            pltpu.VMEM((2, *square), F32),
            pltpu.VMEM((2, *square), BF16),
            pltpu.VMEM((2, *square), BF16),
            pltpu.VMEM((2, *square), BF16),
            pltpu.VMEM(square, BF16),
            pltpu.VMEM(square, F32),
        ],
        27,
        5_000_000_000,
        4_000_000,
    )(place, chunks, factor, other_factor)

    came_back = lax.all_to_all(outgoing.reshape(2, OWNERS, ROWS, COLS), ("pair", "chip"), 1, 1, tiled=True)
    came_back = came_back.reshape(2, ORDER, COLS)
    crossed = lax.ppermute(came_back[1], "core", [(0, 1), (1, 0)])
    (update,) = call(
        place_kernel,
        [SMEM, SMEM, VMEM, VMEM],
        [(VMEM, ((flat, COLS), BF16))],
        [pltpu.VMEM((2, OWNERS // 2, 8, COLS), F32), pltpu.VMEM((BLOCKS + 8, ROWS, COLS), F32)],
        16,
        1_000_000,
        500_000,
    )(table, place, came_back[0], crossed)
    local = (BLOCKS, ROWS, COLS)
    return update.reshape(local), new_first.reshape(local), new_second.reshape(local), new_factor[None, None]


def solution(mesh):
    devices = mesh.devices.reshape(CHIPS, CORES, NARROW // 2, 2)
    rows, cols = ("chip", "core"), ("pair", "side")
    moments = P(None, rows, cols)
    factors = P(rows, cols, None, None)
    return jax.shard_map(
        per_device,
        mesh=Mesh(devices, rows + cols),
        in_specs=(P(cols, None, rows, None), moments, moments, factors, P(), P()),
        out_specs=(moments, moments, moments, factors),
        check_vma=False,
    )
```

```python
import jax
import jax.numpy as jnp
from jax import lax
from jax.experimental import pallas as pl
from jax.experimental.pallas import tpu as pltpu
from jax.sharding import Mesh, PartitionSpec as P

BLOCKS = 192
OWNERS = 128
NARROW = 4
ROWS = 4
COLS = 128
ORDER = 512
CORES = 2
CHIPS = OWNERS // CORES
GROUP = 18
HALF = CHIPS * ROWS
BF16 = jnp.bfloat16
F32 = jnp.float32
VMEM = pl.BlockSpec(memory_space=pltpu.VMEM)
SMEM = pl.BlockSpec(memory_space=pltpu.SMEM)
ANY = pl.BlockSpec(memory_space=pl.ANY)
PAIRS = BLOCKS // 2
EMPTY = BLOCKS
POLY = (1.5625, -1101.25 / 1024.0, 781.25 / 1024.0, -312.5 / 1024.0, 62.5 / 1024.0, -6.25 / 1024.0, 0.25 / 1024.0)


def three_terms(value):
    high = value.astype(BF16).astype(F32)
    rest = value - high
    middle = rest.astype(BF16).astype(F32)
    return high, middle, (rest - middle).astype(BF16).astype(F32)


def columns_kernel(parts, out, sem):
    copies = [
        pltpu.make_async_copy(parts.at[:, :, pl.ds(COLS * n, COLS)], out.at[n], sem.at[n]) for n in range(NARROW)
    ]
    for copy in copies:
        copy.start()
    for copy in copies:
        copy.wait()


def table_kernel(order, counts, table):
    def step(index, start):
        for k in range(8):
            owner = index * 8 + k
            count = counts[owner]
            for slot in range(2):
                block = order[jnp.minimum(start + slot, BLOCKS - 1)]
                filled = count > slot
                half = (block & 1) if slot == 0 else 1 - (block & 1)
                table[slot * OWNERS + owner] = jnp.where(filled, (block >> 1) + PAIRS * half, EMPTY)
                table[(2 + slot) * OWNERS + owner] = jnp.where(filled, block, EMPTY)
            start = start + count
        return start

    lax.fori_loop(0, OWNERS // 8, step, jnp.int32(0))


def moments_kernel(
    table, parts, first, second, new_first, new_second, out, entries, slots, moment_held, variance_held, sem
):
    gradient = jnp.sum(parts[...].astype(F32), axis=0)
    moment = 0.9 * first[...] + 0.1 * gradient
    variance = 0.95 * second[...] + 0.05 * gradient * gradient
    moment_held[...] = moment
    variance_held[...] = variance
    copies = [
        pltpu.make_async_copy(moment_held, new_first, sem.at[0]),
        pltpu.make_async_copy(variance_held, new_second, sem.at[1]),
    ]
    for copy in copies:
        copy.start()
    adam = moment / (jnp.sqrt(variance) + 1e-08)
    gradient = gradient.reshape(PAIRS, 8, COLS)
    entries[:PAIRS, 0:8] = gradient
    entries[PAIRS : 2 * PAIRS, 0:4] = gradient[:, 4:8]
    entries[PAIRS : 2 * PAIRS, 4:8] = gradient[:, 0:4]
    squares = (adam * adam).reshape(PAIRS, 8, COLS)
    upper = lax.broadcasted_iota(jnp.int32, (1, 8, COLS), 1) < ROWS
    wide_lane = lax.broadcasted_iota(jnp.int32, (1, 8, COLS), 2)
    fore = (wide_lane < 3) | ((wide_lane >= 6) & (wide_lane < 9))
    row_sums = jnp.sum(squares, axis=2, keepdims=True)
    lane = lax.broadcasted_iota(jnp.int32, (1, 1, COLS), 2)
    term = sum(jnp.where(lane >= at, -3, 0) for at in (3, 6, 9)) + lane
    for half in range(2):
        pick = (upper == fore) if half == 0 else (upper != fore)
        total = jnp.sum(jnp.where(pick, row_sums, 0.0), axis=1, keepdims=True)
        high, middle, low = three_terms(total)
        pieces = jnp.where(term == 0, high, jnp.where(term == 1, middle, low))
        entries[PAIRS * half : PAIRS * (half + 1), 8:9] = pieces
    entries[EMPTY] = jnp.zeros((16, COLS), F32)
    row = lax.broadcasted_iota(jnp.int32, (8, COLS), 0)
    across = lax.broadcasted_iota(jnp.int32, (1, COLS), 1)

    def four_chips(step, carry):
        base = pl.multiple_of(step * (4 * GROUP), 8)
        for k in range(4):
            at = base + GROUP * k
            totals = []
            for core in range(CORES):
                owner = (step * 4 + k) * CORES + core
                entry0, entry1 = table[owner], table[OWNERS + owner]
                slots[pl.ds(at + 8 * core, 8)] = jnp.where(row < ROWS, entries[entry0, 0:8], entries[entry1, 0:8])
                totals += [entries[entry0, 8:9], entries[entry1, 8:9]]
            first_owner = jnp.where(across < 3, totals[0], totals[1])
            second_owner = jnp.where(across < 9, totals[2], totals[3])
            totals = jnp.where(across < 6, first_owner, second_owner)
            slots[pl.ds(at + 16, 2)] = jnp.broadcast_to(totals, (2, COLS))
        return carry

    lax.fori_loop(0, CHIPS // 4, four_chips, 0)
    out[...] = slots[...].astype(BF16)
    for copy in copies:
        copy.wait()


def spread_kernel(arrived, out):
    groups = arrived[...].astype(F32).reshape(CHIPS // 4, 4 * GROUP, COLS)
    starts = [GROUP * k for k in range(4)]
    total = jnp.sum(sum(groups[:, at + 16 : at + 17] for at in starts), axis=0)
    across = lax.broadcasted_iota(jnp.int32, (1, COLS), 1)
    for core in range(CORES):
        for slot in range(2):
            place = 2 * core + slot
            rows = [groups[:, at + ROWS * place : at + ROWS * (place + 1)] for at in starts]
            block = jnp.concatenate(rows, axis=1).reshape(HALF, COLS).astype(BF16)
            mine = (across >= 3 * place) & (across < 3 * place + 3)
            sum_sq = jnp.sum(jnp.where(mine, total, 0.0), axis=1, keepdims=True)
            high, middle, low = three_terms(jnp.broadcast_to(sum_sq, (1, COLS)))
            pieces = jnp.where(across == 0, high, jnp.where(across == 1, middle, jnp.where(across == 2, low, 0.0)))
            pieces = jnp.broadcast_to(pieces, (16, COLS)).astype(BF16)
            for member in (2 * slot, 2 * slot + 1):
                out[NARROW * core + member, 0:HALF] = block
                out[NARROW * core + member, HALF : HALF + 16] = pieces


def product(left, right, contract=((1,), (0,))):
    return lax.dot_general(left, right, (contract, ((), ())), preferred_element_type=F32)


def two_terms(value):
    high = value.astype(BF16)
    return high, (value - high.astype(F32)).astype(BF16)


def sum_of_squares(parts):
    total = sum(jnp.sum((part * part).reshape(-1, 8, ORDER), axis=0) for part in parts)
    return jnp.sum(jnp.sum(total, axis=0, keepdims=True), axis=1, keepdims=True)


def owner_kernel(
    place_ref, chunks, mine, other, new_mine, outgoing, grad, stats, lefts, rights, later, squares, outer, cubes, roots, inner, result
):
    here, core = place_ref[0], place_ref[1]
    is_right = here == 1
    halves = [slice(0, ORDER // 2), slice(ORDER // 2, ORDER)]
    for n in range(NARROW):
        rows = [chunks[NARROW * core + n, 0:HALF].astype(F32).reshape(CHIPS, ROWS, COLS) for core in range(CORES)]
        grad[:, COLS * n : COLS * (n + 1)] = jnp.concatenate(rows, axis=1).reshape(ORDER, COLS).astype(BF16)
    adam_sq = sum(chunks[k, HALF : HALF + 16].astype(F32)[0:1] for k in range(CORES * NARROW))
    adam_sq = jnp.sum(adam_sq, axis=1, keepdims=True)

    def statistics(left_factor, right_factor, side):
        for rows in halves:
            left = 0.9 * left_factor[rows].astype(F32) + 0.1 * product(grad[rows], grad[...], ((1,), (1,)))
            stats[0, rows] = left
            if side == 0:
                new_mine[rows] = left
        for rows in halves:
            right = 0.9 * right_factor[rows].astype(F32) + 0.1 * product(grad[:, rows], grad[...], ((0,), (0,)))
            stats[1, rows] = right
            if side == 1:
                new_mine[rows] = right

    @pl.when(jnp.logical_not(is_right))
    def _():
        statistics(mine, other, 0)

    @pl.when(is_right)
    def _():
        statistics(other, mine, 1)

    norms = [jnp.sqrt(sum_of_squares([stats[side, rows] for rows in halves])) for side in range(2)]
    inverses = [1.0 / norm for norm in norms]

    def put_right(target, side, rows, high, low):
        for third, term in enumerate((high, low, high)):
            target[side, third * ORDER + rows.start : third * ORDER + rows.stop] = term

    for side in range(2):
        for rows in halves:
            high, low = two_terms(stats[side, rows] * inverses[side])
            for third, term in enumerate((high, high, low)):
                lefts[side, rows, third * ORDER : (third + 1) * ORDER] = term
            put_right(rights, side, rows, high, low)
    for side in range(2):
        for rows in halves:
            square = product(lefts[side, rows], rights[side])
            squares[side, rows] = square
            put_right(later, side, rows, *two_terms(square))
    for side in range(2):
        for rows in halves:
            cube = product(lefts[side, rows], later[side])
            matrix = stats[side, rows] * inverses[side]
            square = squares[side, rows]
            outer[side, rows] = (POLY[4] * matrix + POLY[5] * square + POLY[6] * cube).astype(BF16)
            cubes[side, rows] = cube.astype(BF16)
            row = lax.broadcasted_iota(jnp.int32, (ORDER // 2, ORDER), 0) + rows.start
            col = lax.broadcasted_iota(jnp.int32, (ORDER // 2, ORDER), 1)
            value = POLY[1] * matrix + POLY[2] * square + POLY[3] * cube
            squares[side, rows] = value + jnp.where(row == col, POLY[0], 0.0)
    for side in range(2):
        scale = lax.rsqrt(jnp.sqrt(norms[side]))
        for rows in halves:
            value = squares[side, rows] + product(cubes[side, rows], outer[side])
            roots[side, rows] = (value * scale).astype(BF16)
    for rows in halves:
        inner[rows] = product(grad[rows], roots[1]).astype(BF16)
    for rows in halves:
        result[rows] = product(roots[0, rows], inner[...])
    square = sum_of_squares([result[rows] for rows in halves])
    scale = jnp.sqrt(adam_sq) / (jnp.sqrt(square) + 1e-06)
    for pair in range(2):
        cols = result[:, pl.ds(pl.multiple_of((2 * pair + here) * COLS, COLS), COLS)] * scale
        cols = cols.reshape(CHIPS, CORES * ROWS, COLS)
        lower, upper = cols[:, 0:ROWS], cols[:, ROWS : 2 * ROWS]
        staying = jnp.where(core == 0, lower, upper).reshape(HALF, COLS)
        crossing = jnp.where(core == 0, upper, lower).reshape(HALF, COLS)
        outgoing[0, pair * HALF : (pair + 1) * HALF] = staying.astype(BF16)
        outgoing[1, pair * HALF : (pair + 1) * HALF] = crossing.astype(BF16)


def place_kernel(table, place_ref, stayed, crossed, update, wide, blocks):
    wide[0] = stayed[...].astype(F32).reshape(OWNERS // 2, 8, COLS)
    wide[1] = crossed[...].astype(F32).reshape(OWNERS // 2, 8, COLS)
    here = place_ref[1]

    def four_chips(step, carry):
        for k in range(4):
            for core in range(CORES):
                for slot in range(2):
                    block = table[(2 + slot) * OWNERS + (step * 4 + k) * CORES + core]
                    group = slot * (CHIPS // 2) + step * 2 + k // 2
                    first_row = ROWS * (k % 2)
                    blocks[block] = wide[core ^ here, group, first_row : first_row + ROWS]
        return carry

    lax.fori_loop(0, CHIPS // 4, four_chips, 0)
    update[...] = blocks[0:BLOCKS].reshape(BLOCKS * ROWS, COLS).astype(BF16)


def call(kernel, in_specs, outs, scratch, vmem_mib, flops, moved):
    specs, shapes = zip(*outs)
    return pl.pallas_call(
        kernel,
        in_specs=in_specs,
        out_specs=list(specs),
        out_shape=[jax.ShapeDtypeStruct(*shape) for shape in shapes],
        scratch_shapes=scratch,
        compiler_params=pltpu.CompilerParams(vmem_limit_bytes=vmem_mib * 1024 * 1024),
        cost_estimate=pl.CostEstimate(flops=flops, bytes_accessed=moved, transcendentals=0),
    )


def per_device(grad_parts, first_moment, second_moment, factors, block_order, owner_counts):
    place = jnp.stack([lax.axis_index("side"), lax.axis_index("core")]).astype(jnp.int32)
    flat = BLOCKS * ROWS

    (partial_cols,) = call(
        columns_kernel,
        [ANY],
        [(VMEM, ((NARROW, BLOCKS, ROWS, COLS), BF16))],
        [pltpu.SemaphoreType.DMA((NARROW,))],
        16,
        0,
        1_600_000,
    )(grad_parts[0])
    partial_cols, block_order, owner_counts, place = lax.optimization_barrier(
        (partial_cols, block_order, owner_counts, place)
    )
    (table,) = call(table_kernel, [SMEM, SMEM], [(SMEM, ((4 * OWNERS,), jnp.int32))], [], 16, 0, 8_000_000)(
        block_order, owner_counts
    )
    partial_cols = lax.all_to_all(partial_cols, ("pair", "side"), 0, 0, tiled=True)

    factor, partial_cols = lax.optimization_barrier((factors[0, 0], partial_cols))
    other_factor = lax.ppermute(factor.astype(BF16), "side", [(0, 1), (1, 0)])

    new_first, new_second, outgoing = call(
        moments_kernel,
        [SMEM, VMEM, VMEM, VMEM],
        [(ANY, ((flat, COLS), F32)), (ANY, ((flat, COLS), F32)), (VMEM, ((CHIPS * GROUP, COLS), BF16))],
        [
            pltpu.VMEM((BLOCKS + 1, 16, COLS), F32),
            pltpu.VMEM((CHIPS * GROUP, COLS), F32),
            pltpu.VMEM((flat, COLS), F32),
            pltpu.VMEM((flat, COLS), F32),
            pltpu.SemaphoreType.DMA((2,)),
        ],
        16,
        4_000_000,
        2_800_000,
    )(
        table,
        partial_cols.reshape(NARROW, flat, COLS),
        first_moment.reshape(flat, COLS),
        second_moment.reshape(flat, COLS),
    )

    arrived = lax.all_to_all(outgoing.reshape(CHIPS, GROUP // 2, 2, COLS), "chip", 0, 0, tiled=True)
    (spread,) = call(
        spread_kernel,
        [VMEM],
        [(VMEM, ((CORES * NARROW, HALF + 16, COLS), BF16))],
        [],
        16,
        1_000_000,
        900_000,
    )(arrived.reshape(CHIPS * GROUP, COLS))
    spread, other_factor = lax.optimization_barrier((spread, other_factor))
    chunks = lax.all_to_all(spread, ("core", "pair", "side"), 0, 0, tiled=True)

    square = (ORDER, ORDER)
    new_factor, outgoing = call(
        owner_kernel,
        [SMEM, VMEM, VMEM, VMEM],
        [(VMEM, (square, F32)), (VMEM, ((2, ORDER, COLS), BF16))],
        [
            pltpu.VMEM(square, BF16),
            pltpu.VMEM((2, *square), F32),
            pltpu.VMEM((2, ORDER, 3 * ORDER), BF16),
            pltpu.VMEM((2, 3 * ORDER, ORDER), BF16),
            pltpu.VMEM((2, 3 * ORDER, ORDER), BF16),
            pltpu.VMEM((2, *square), F32),
            pltpu.VMEM((2, *square), BF16),
            pltpu.VMEM((2, *square), BF16),
            pltpu.VMEM((2, *square), BF16),
            pltpu.VMEM(square, BF16),
            pltpu.VMEM(square, F32),
        ],
        27,
        5_000_000_000,
        4_000_000,
    )(place, chunks, factor, other_factor)

    came_back = lax.all_to_all(outgoing.reshape(2, OWNERS, ROWS, COLS), ("pair", "chip"), 1, 1, tiled=True)
    came_back = came_back.reshape(2, ORDER, COLS)
    crossed = lax.ppermute(came_back[1], "core", [(0, 1), (1, 0)])
    (update,) = call(
        place_kernel,
        [SMEM, SMEM, VMEM, VMEM],
        [(VMEM, ((flat, COLS), BF16))],
        [pltpu.VMEM((2, OWNERS // 2, 8, COLS), F32), pltpu.VMEM((BLOCKS + 8, ROWS, COLS), F32)],
        16,
        1_000_000,
        500_000,
    )(table, place, came_back[0], crossed)
    local = (BLOCKS, ROWS, COLS)
    return update.reshape(local), new_first.reshape(local), new_second.reshape(local), new_factor[None, None]


def solution(mesh):
    devices = mesh.devices.reshape(CHIPS, CORES, NARROW // 2, 2)
    rows, cols = ("chip", "core"), ("pair", "side")
    moments = P(None, rows, cols)
    factors = P(rows, cols, None, None)
    return jax.shard_map(
        per_device,
        mesh=Mesh(devices, rows + cols),
        in_specs=(P(cols, None, rows, None), moments, moments, factors, P(), P()),
        out_specs=(moments, moments, moments, factors),
        check_vma=False,
    )
```

```python
import jax
import jax.numpy as jnp
from jax import lax
from jax.experimental import pallas as pl
from jax.experimental.pallas import tpu as pltpu
from jax.sharding import Mesh, PartitionSpec as P

BLOCKS = 192
OWNERS = 128
NARROW = 4
ROWS = 4
COLS = 128
ORDER = 512
CORES = 2
CHIPS = OWNERS // CORES
GROUP = 18
HALF = CHIPS * ROWS
BF16 = jnp.bfloat16
F32 = jnp.float32
VMEM = pl.BlockSpec(memory_space=pltpu.VMEM)
SMEM = pl.BlockSpec(memory_space=pltpu.SMEM)
ANY = pl.BlockSpec(memory_space=pl.ANY)
PAIRS = BLOCKS // 2
EMPTY = BLOCKS
POLY = (1.5625, -1101.25 / 1024.0, 781.25 / 1024.0, -312.5 / 1024.0, 62.5 / 1024.0, -6.25 / 1024.0, 0.25 / 1024.0)


def three_terms(value):
    high = value.astype(BF16).astype(F32)
    rest = value - high
    middle = rest.astype(BF16).astype(F32)
    return high, middle, (rest - middle).astype(BF16).astype(F32)


def columns_kernel(parts, out, sem):
    copies = [
        pltpu.make_async_copy(parts.at[:, :, pl.ds(COLS * n, COLS)], out.at[n], sem.at[n]) for n in range(NARROW)
    ]
    for copy in copies:
        copy.start()
    for copy in copies:
        copy.wait()


def table_kernel(order, counts, table):
    def step(index, start):
        for k in range(8):
            owner = index * 8 + k
            count = counts[owner]
            for slot in range(2):
                block = order[jnp.minimum(start + slot, BLOCKS - 1)]
                filled = count > slot
                half = (block & 1) if slot == 0 else 1 - (block & 1)
                table[slot * OWNERS + owner] = jnp.where(filled, (block >> 1) + PAIRS * half, EMPTY)
                table[(2 + slot) * OWNERS + owner] = jnp.where(filled, block, EMPTY)
            start = start + count
        return start

    lax.fori_loop(0, OWNERS // 8, step, jnp.int32(0))


def moments_kernel(
    table, parts, first, second, new_first, new_second, out, entries, slots, moment_held, variance_held, sem
):
    gradient = jnp.sum(parts[...].astype(F32), axis=0)
    moment = 0.9 * first[...] + 0.1 * gradient
    variance = 0.95 * second[...] + 0.05 * gradient * gradient
    moment_held[...] = moment
    variance_held[...] = variance
    copies = [
        pltpu.make_async_copy(moment_held, new_first, sem.at[0]),
        pltpu.make_async_copy(variance_held, new_second, sem.at[1]),
    ]
    for copy in copies:
        copy.start()
    adam = moment / (jnp.sqrt(variance) + 1e-08)
    gradient = gradient.reshape(PAIRS, 8, COLS)
    entries[:PAIRS, 0:8] = gradient
    entries[PAIRS : 2 * PAIRS, 0:4] = gradient[:, 4:8]
    entries[PAIRS : 2 * PAIRS, 4:8] = gradient[:, 0:4]
    squares = (adam * adam).reshape(PAIRS, 8, COLS)
    upper = lax.broadcasted_iota(jnp.int32, (1, 8, COLS), 1) < ROWS
    wide_lane = lax.broadcasted_iota(jnp.int32, (1, 8, COLS), 2)
    fore = (wide_lane < 3) | ((wide_lane >= 6) & (wide_lane < 9))
    row_sums = jnp.sum(squares, axis=2, keepdims=True)
    lane = lax.broadcasted_iota(jnp.int32, (1, 1, COLS), 2)
    term = sum(jnp.where(lane >= at, -3, 0) for at in (3, 6, 9)) + lane
    for half in range(2):
        pick = (upper == fore) if half == 0 else (upper != fore)
        total = jnp.sum(jnp.where(pick, row_sums, 0.0), axis=1, keepdims=True)
        high, middle, low = three_terms(total)
        pieces = jnp.where(term == 0, high, jnp.where(term == 1, middle, low))
        entries[PAIRS * half : PAIRS * (half + 1), 8:9] = pieces
    entries[EMPTY] = jnp.zeros((16, COLS), F32)
    row = lax.broadcasted_iota(jnp.int32, (8, COLS), 0)
    across = lax.broadcasted_iota(jnp.int32, (1, COLS), 1)

    def four_chips(step, carry):
        base = pl.multiple_of(step * (4 * GROUP), 8)
        for k in range(4):
            at = base + GROUP * k
            totals = []
            for core in range(CORES):
                owner = (step * 4 + k) * CORES + core
                entry0, entry1 = table[owner], table[OWNERS + owner]
                slots[pl.ds(at + 8 * core, 8)] = jnp.where(row < ROWS, entries[entry0, 0:8], entries[entry1, 0:8])
                totals += [entries[entry0, 8:9], entries[entry1, 8:9]]
            first_owner = jnp.where(across < 3, totals[0], totals[1])
            second_owner = jnp.where(across < 9, totals[2], totals[3])
            totals = jnp.where(across < 6, first_owner, second_owner)
            slots[pl.ds(at + 16, 2)] = jnp.broadcast_to(totals, (2, COLS))
        return carry

    lax.fori_loop(0, CHIPS // 4, four_chips, 0)
    out[...] = slots[...].astype(BF16)
    for copy in copies:
        copy.wait()


def spread_kernel(arrived, out):
    groups = arrived[...].astype(F32).reshape(CHIPS // 4, 4 * GROUP, COLS)
    starts = [GROUP * k for k in range(4)]
    total = jnp.sum(sum(groups[:, at + 16 : at + 17] for at in starts), axis=0)
    across = lax.broadcasted_iota(jnp.int32, (1, COLS), 1)
    for core in range(CORES):
        for slot in range(2):
            place = 2 * core + slot
            rows = [groups[:, at + ROWS * place : at + ROWS * (place + 1)] for at in starts]
            block = jnp.concatenate(rows, axis=1).reshape(HALF, COLS).astype(BF16)
            mine = (across >= 3 * place) & (across < 3 * place + 3)
            sum_sq = jnp.sum(jnp.where(mine, total, 0.0), axis=1, keepdims=True)
            high, middle, low = three_terms(jnp.broadcast_to(sum_sq, (1, COLS)))
            pieces = jnp.where(across == 0, high, jnp.where(across == 1, middle, jnp.where(across == 2, low, 0.0)))
            pieces = jnp.broadcast_to(pieces, (16, COLS)).astype(BF16)
            for member in (2 * slot, 2 * slot + 1):
                out[NARROW * core + member, 0:HALF] = block
                out[NARROW * core + member, HALF : HALF + 16] = pieces


def product(left, right, contract=((1,), (0,))):
    return lax.dot_general(left, right, (contract, ((), ())), preferred_element_type=F32)


def two_terms(value):
    high = value.astype(BF16)
    return high, (value - high.astype(F32)).astype(BF16)


def sum_of_squares(parts):
    total = sum(jnp.sum((part * part).reshape(-1, 8, ORDER), axis=0) for part in parts)
    return jnp.sum(jnp.sum(total, axis=0, keepdims=True), axis=1, keepdims=True)


def owner_kernel(
    place_ref, chunks, mine, other, new_mine, outgoing, grad, stats, lefts, rights, later, squares, outer, cubes, roots, inner, result
):
    core, front = place_ref[1], place_ref[2]
    is_right = place_ref[0] == 1
    halves = [slice(0, ORDER // 2), slice(ORDER // 2, ORDER)]
    for n in range(NARROW):
        rows = [chunks[NARROW * core + n, 0:HALF].astype(F32).reshape(CHIPS, ROWS, COLS) for core in range(CORES)]
        grad[:, COLS * n : COLS * (n + 1)] = jnp.concatenate(rows, axis=1).reshape(ORDER, COLS).astype(BF16)
    adam_sq = sum(chunks[k, HALF : HALF + 16].astype(F32)[0:1] for k in range(CORES * NARROW))
    adam_sq = jnp.sum(adam_sq, axis=1, keepdims=True)

    def statistics(left_factor, right_factor, side):
        for rows in halves:
            left = 0.9 * left_factor[rows].astype(F32) + 0.1 * product(grad[rows], grad[...], ((1,), (1,)))
            stats[0, rows] = left
            if side == 0:
                new_mine[rows] = left
        for rows in halves:
            right = 0.9 * right_factor[rows].astype(F32) + 0.1 * product(grad[:, rows], grad[...], ((0,), (0,)))
            stats[1, rows] = right
            if side == 1:
                new_mine[rows] = right

    @pl.when(jnp.logical_not(is_right))
    def _():
        statistics(mine, other, 0)

    @pl.when(is_right)
    def _():
        statistics(other, mine, 1)

    norms = [jnp.sqrt(sum_of_squares([stats[side, rows] for rows in halves])) for side in range(2)]
    inverses = [1.0 / norm for norm in norms]

    def put_right(target, side, rows, high, low):
        for third, term in enumerate((high, low, high)):
            target[side, third * ORDER + rows.start : third * ORDER + rows.stop] = term

    for side in range(2):
        for rows in halves:
            high, low = two_terms(stats[side, rows] * inverses[side])
            for third, term in enumerate((high, high, low)):
                lefts[side, rows, third * ORDER : (third + 1) * ORDER] = term
            put_right(rights, side, rows, high, low)
    for side in range(2):
        for rows in halves:
            square = product(lefts[side, rows], rights[side])
            squares[side, rows] = square
            put_right(later, side, rows, *two_terms(square))
    for side in range(2):
        for rows in halves:
            cube = product(lefts[side, rows], later[side])
            matrix = stats[side, rows] * inverses[side]
            square = squares[side, rows]
            outer[side, rows] = (POLY[4] * matrix + POLY[5] * square + POLY[6] * cube).astype(BF16)
            cubes[side, rows] = cube.astype(BF16)
            row = lax.broadcasted_iota(jnp.int32, (ORDER // 2, ORDER), 0) + rows.start
            col = lax.broadcasted_iota(jnp.int32, (ORDER // 2, ORDER), 1)
            value = POLY[1] * matrix + POLY[2] * square + POLY[3] * cube
            squares[side, rows] = value + jnp.where(row == col, POLY[0], 0.0)
    for side in range(2):
        scale = lax.rsqrt(jnp.sqrt(norms[side]))
        for rows in halves:
            value = squares[side, rows] + product(cubes[side, rows], outer[side])
            roots[side, rows] = (value * scale).astype(BF16)
    for rows in halves:
        inner[rows] = product(grad[rows], roots[1]).astype(BF16)
    for rows in halves:
        result[rows] = product(roots[0, rows], inner[...])
    square = sum_of_squares([result[rows] for rows in halves])
    scale = jnp.sqrt(adam_sq) / (jnp.sqrt(square) + 1e-06)
    for pair in range(2):
        member = front if pair == 0 else NARROW - 1 - front
        cols = result[:, pl.ds(pl.multiple_of(member * COLS, COLS), COLS)] * scale
        cols = cols.reshape(CHIPS, CORES * ROWS, COLS)
        lower, upper = cols[:, 0:ROWS], cols[:, ROWS : 2 * ROWS]
        staying = jnp.where(core == 0, lower, upper).reshape(HALF, COLS)
        crossing = jnp.where(core == 0, upper, lower).reshape(HALF, COLS)
        outgoing[0, pair * HALF : (pair + 1) * HALF] = staying.astype(BF16)
        outgoing[1, pair * HALF : (pair + 1) * HALF] = crossing.astype(BF16)


def place_kernel(table, place_ref, stayed, crossed, update, wide, blocks):
    wide[0] = stayed[...].astype(F32).reshape(OWNERS // 2, 8, COLS)
    wide[1] = crossed[...].astype(F32).reshape(OWNERS // 2, 8, COLS)
    here = place_ref[1]

    def four_chips(step, carry):
        for k in range(4):
            for core in range(CORES):
                for slot in range(2):
                    block = table[(2 + slot) * OWNERS + (step * 4 + k) * CORES + core]
                    group = slot * (CHIPS // 2) + step * 2 + k // 2
                    first_row = ROWS * (k % 2)
                    blocks[block] = wide[core ^ here, group, first_row : first_row + ROWS]
        return carry

    lax.fori_loop(0, CHIPS // 4, four_chips, 0)
    update[...] = blocks[0:BLOCKS].reshape(BLOCKS * ROWS, COLS).astype(BF16)


def call(kernel, in_specs, outs, scratch, vmem_mib, flops, moved):
    specs, shapes = zip(*outs)
    return pl.pallas_call(
        kernel,
        in_specs=in_specs,
        out_specs=list(specs),
        out_shape=[jax.ShapeDtypeStruct(*shape) for shape in shapes],
        scratch_shapes=scratch,
        compiler_params=pltpu.CompilerParams(vmem_limit_bytes=vmem_mib * 1024 * 1024),
        cost_estimate=pl.CostEstimate(flops=flops, bytes_accessed=moved, transcendentals=0),
    )


def per_device(grad_parts, first_moment, second_moment, factors, block_order, owner_counts):
    pair, side, core = (lax.axis_index(name) for name in ("pair", "side", "core"))
    front = jnp.where(pair == 0, side, 1 - side)
    place = jnp.stack([side, core, front]).astype(jnp.int32)
    index = [[member * CHIPS + chip for chip in range(CHIPS)] for member in range(NARROW)]
    sharing = [index[0] + index[3], index[1] + index[2]]
    flat = BLOCKS * ROWS

    (partial_cols,) = call(
        columns_kernel,
        [ANY],
        [(VMEM, ((NARROW, BLOCKS, ROWS, COLS), BF16))],
        [pltpu.SemaphoreType.DMA((NARROW,))],
        16,
        0,
        1_600_000,
    )(grad_parts[0])
    partial_cols, block_order, owner_counts, place = lax.optimization_barrier(
        (partial_cols, block_order, owner_counts, place)
    )
    (table,) = call(table_kernel, [SMEM, SMEM], [(SMEM, ((4 * OWNERS,), jnp.int32))], [], 16, 0, 8_000_000)(
        block_order, owner_counts
    )
    partial_cols = lax.all_to_all(partial_cols, ("pair", "side"), 0, 0, tiled=True)

    factor, partial_cols = lax.optimization_barrier((factors[0, 0], partial_cols))
    other_factor = lax.ppermute(factor.astype(BF16), "side", [(0, 1), (1, 0)])

    new_first, new_second, outgoing = call(
        moments_kernel,
        [SMEM, VMEM, VMEM, VMEM],
        [(ANY, ((flat, COLS), F32)), (ANY, ((flat, COLS), F32)), (VMEM, ((CHIPS * GROUP, COLS), BF16))],
        [
            pltpu.VMEM((BLOCKS + 1, 16, COLS), F32),
            pltpu.VMEM((CHIPS * GROUP, COLS), F32),
            pltpu.VMEM((flat, COLS), F32),
            pltpu.VMEM((flat, COLS), F32),
            pltpu.SemaphoreType.DMA((2,)),
        ],
        16,
        4_000_000,
        2_800_000,
    )(
        table,
        partial_cols.reshape(NARROW, flat, COLS),
        first_moment.reshape(flat, COLS),
        second_moment.reshape(flat, COLS),
    )

    arrived = lax.all_to_all(outgoing.reshape(CHIPS, GROUP // 2, 2, COLS), "chip", 0, 0, tiled=True)
    (spread,) = call(
        spread_kernel,
        [VMEM],
        [(VMEM, ((CORES * NARROW, HALF + 16, COLS), BF16))],
        [],
        16,
        1_000_000,
        900_000,
    )(arrived.reshape(CHIPS * GROUP, COLS))
    spread, other_factor = lax.optimization_barrier((spread, other_factor))
    chunks = lax.all_to_all(spread, ("core", "pair", "side"), 0, 0, tiled=True)

    square = (ORDER, ORDER)
    new_factor, outgoing = call(
        owner_kernel,
        [SMEM, VMEM, VMEM, VMEM],
        [(VMEM, (square, F32)), (VMEM, ((2, ORDER, COLS), BF16))],
        [
            pltpu.VMEM(square, BF16),
            pltpu.VMEM((2, *square), F32),
            pltpu.VMEM((2, ORDER, 3 * ORDER), BF16),
            pltpu.VMEM((2, 3 * ORDER, ORDER), BF16),
            pltpu.VMEM((2, 3 * ORDER, ORDER), BF16),
            pltpu.VMEM((2, *square), F32),
            pltpu.VMEM((2, *square), BF16),
            pltpu.VMEM((2, *square), BF16),
            pltpu.VMEM((2, *square), BF16),
            pltpu.VMEM(square, BF16),
            pltpu.VMEM(square, F32),
        ],
        27,
        5_000_000_000,
        4_000_000,
    )(place, chunks, factor, other_factor)

    came_back = lax.all_to_all(
        outgoing.reshape(2, OWNERS, ROWS, COLS),
        ("pair", "side", "chip"),
        1,
        1,
        axis_index_groups=sharing,
        tiled=True,
    )
    came_back = came_back.reshape(2, ORDER, COLS)
    crossed = lax.ppermute(came_back[1], "core", [(0, 1), (1, 0)])
    (update,) = call(
        place_kernel,
        [SMEM, SMEM, VMEM, VMEM],
        [(VMEM, ((flat, COLS), BF16))],
        [pltpu.VMEM((2, OWNERS // 2, 8, COLS), F32), pltpu.VMEM((BLOCKS + 8, ROWS, COLS), F32)],
        16,
        1_000_000,
        500_000,
    )(table, place, came_back[0], crossed)
    local = (BLOCKS, ROWS, COLS)
    return update.reshape(local), new_first.reshape(local), new_second.reshape(local), new_factor[None, None]


def solution(mesh):
    devices = mesh.devices.reshape(CHIPS, CORES, NARROW // 2, 2)
    rows, cols = ("chip", "core"), ("pair", "side")
    moments = P(None, rows, cols)
    factors = P(rows, cols, None, None)
    return jax.shard_map(
        per_device,
        mesh=Mesh(devices, rows + cols),
        in_specs=(P(cols, None, rows, None), moments, moments, factors, P(), P()),
        out_specs=(moments, moments, moments, factors),
        check_vma=False,
    )
```
